32 devices in a mesh: groups: 2 (over y), ctx: 4 (over z), tm: 2 (over x), tp: 2 (over core).
Axes of the slice: x: 2, y: 2, z: 4, core: 2. Of those that a mesh axis runs over, the one named last changes fastest.
Arguments:
- tokens: bfloat16 [256, 8, 1024], P(('groups', 'tm'), 'ctx'), parts along dimension 0, may hold values from -6 to 6
- norm_gain: float32 [1024], replicated, may hold values from 0.1 to 1.9
- block_mask: int32 [4, 4, 4], P(('groups', 'tm'), 'ctx'), parts along dimension 0, may hold values from 0 to 1, as said below
- w_query: bfloat16 [1024, 1024], P('tm', 'tp'), may hold values from -1.25 to 1.25
- w_key: bfloat16 [1024, 1024], P('tm', 'tp'), may hold values from -1.25 to 1.25
- w_value: bfloat16 [1024, 1024], P('tm', 'tp'), may hold values from -0.1875 to 0.1875
- w_out: bfloat16 [1024, 1024], P('tp', 'tm'), may hold values from -0.1875 to 0.1875
- w_up: bfloat16 [1024, 2048], P('tm', 'tp'), may hold values from -0.1875 to 0.1875
- w_down: bfloat16 [2048, 1024], P('tp', 'tm'), may hold values from -0.125 to 0.125
- conv_weight: float32 [5, 1024], P(None, 'tp'), may hold values from -2.5 to 2.5
Outputs:
- denoised: bfloat16 [256, 8, 1024], P(('groups', 'tm'), 'ctx', 'tp'), parts along dimension 0
The draws below stay inside these ranges and needn't reach their ends.
There are 2 independent parts, one for each index of `groups`. The reference program is written for one: setup_inputs(seed, part) draws one part's arguments, and reference() takes and returns one part's arrays. A program takes and returns all parts, laid end to end along the dimension named above; an argument that names none is the same for every part. Nothing has to cross between parts.
Inputs may be any that keep to these rules, and one draw needn't show every extreme that they name: block_mask[w, i, i] is 1 for every window w and block i.
All inputs are finite; a program needn't handle non-finite values.
Results may differ from the reference program's by a relative error of at most 0.0076.
Values may be sent and summed in bfloat16 or wider, within the bound.
No kernel may reach another device: no remote copies, remote signals or barrier semaphores. Data moves between devices by JAX's collectives and lax.ppermute only.
A program may use at most 64 MiB of HBM per device.

```python
import jax
import jax.numpy as jnp
from jax import lax

D = 1024
HEADS = 16
HEAD_DIM = 64
FF = 2048
KERNEL = 5
DAN_DEV = 2
FRAME_DEV = 64
DANCERS = 8
FRAMES = 128
N_CTX = 4
N_TM = 2


def draw_block_mask(key, part):
    first = jax.random.fold_in(key, 11)
    second = jax.random.fold_in(key, 23)
    levels = jax.random.randint(first, (N_TM, N_CTX, 1), 1, 10)
    rolls = jax.random.randint(second, (N_TM, N_CTX, N_CTX), 0, 10)
    allowed = (rolls < levels).astype(jnp.int32)
    diagonal = jnp.eye(N_CTX, dtype=jnp.int32)[None, :, :]
    return jnp.maximum(allowed, diagonal)


def draw_tokens(key, part):
    noise = jax.random.normal(jax.random.fold_in(key, 7), (FRAMES, DANCERS, D), jnp.float32)
    return jnp.clip(noise, -6.0, 6.0).astype(jnp.bfloat16)


def drawn_weight(key, salt):
    scale = D ** (-0.5)
    drawn = jax.random.normal(jax.random.fold_in(key, salt), (D, D), jnp.float32)
    return jnp.clip(drawn * scale, -6.0 * scale, 6.0 * scale)


def draw_w_query(key, part):
    return drawn_weight(key, 201).astype(jnp.bfloat16)


def draw_w_key(key, part):
    return drawn_weight(key, 202).astype(jnp.bfloat16)


def level_of(key, dims, cuts, low, largest):
    def one(position, blocks):
        steps = jax.random.uniform(jax.random.fold_in(jax.random.fold_in(key, 6), position), (blocks,), jnp.float32, low / len(cuts), largest / len(cuts))
        return jnp.repeat(jnp.exp(steps), dims[position] // blocks).reshape((-1,) + (1,) * (len(dims) - position - 1))

    level = one(*cuts[0])
    for cut in cuts[1:]:
        level = level * one(*cut)
    return level


def scatter_about(own_key, shape, spread, reach, split=(), held_as=jnp.bfloat16):
    values = jax.random.normal(own_key, shape, jnp.float32) * spread
    if len(split) > 0:
        values = level_of(own_key, shape, split, -0.22, 0.18) * values
    return jnp.clip(values, min=-reach, max=reach).astype(held_as)


def setup_inputs(seed: int = 0, part: int = 0) -> dict:
    key_of = jax.random.split(jax.random.key(seed), 11)
    own_keys = jax.random.split(jax.random.fold_in(key_of[10], part), 11)
    return {
        "tokens": draw_tokens(jax.random.fold_in(jax.random.fold_in(key_of[10], part), 71), part),
        "norm_gain": jnp.clip(1.0 + 0.18 * jax.random.normal(key_of[1], (D,), jnp.float32), 0.1, 1.9),
        "block_mask": draw_block_mask(jax.random.fold_in(jax.random.fold_in(key_of[10], part), 71), part),
        "w_query": draw_w_query(jax.random.fold_in(key_of[10], 71), part),
        "w_key": draw_w_key(jax.random.fold_in(key_of[10], 71), part),
        "w_value": scatter_about(key_of[5], (D, D), D ** -0.5, 0.1875, ((0, 2), (1, 2))),
        "w_out": scatter_about(key_of[6], (D, D), D ** -0.5, 0.1875, ((0, 2), (1, 2))),
        "w_up": scatter_about(key_of[7], (D, FF), D ** -0.5, 0.1875, ((0, 2), (1, 2))),
        "w_down": scatter_about(key_of[8], (FF, D), FF ** -0.5, 0.125, ((0, 2), (1, 2))),
        "conv_weight": scatter_about(key_of[9], (KERNEL, D), KERNEL ** -0.5, 2.5, ((1, 2),), jnp.float32),
    }


def rms_norm(tokens, norm_gain):
    values = tokens.astype(jnp.float32)
    square = lax.optimization_barrier(jnp.mean(values * values, axis=-1, keepdims=True))
    return (values * lax.rsqrt(square + 1e-05) * norm_gain).astype(jnp.bfloat16)

def reference(tokens, norm_gain, block_mask, w_query, w_key, w_value, w_out, w_up, w_down, conv_weight):
    normed = rms_norm(tokens, norm_gain)
    flat = normed.reshape(FRAMES * DANCERS, D)
    queries = jnp.dot(flat, w_query, preferred_element_type=jnp.float32).astype(jnp.bfloat16)
    keys = jnp.dot(flat, w_key, preferred_element_type=jnp.float32).astype(jnp.bfloat16)
    values = jnp.dot(flat, w_value, preferred_element_type=jnp.float32).astype(jnp.bfloat16)
    window_tokens = FRAME_DEV * DANCERS

    def split_heads(array):
        return array.reshape(N_TM, window_tokens, HEADS, HEAD_DIM).transpose(0, 2, 1, 3)
    blocks = jnp.arange(DANCERS) // DAN_DEV
    chooser = (blocks[:, None] == jnp.arange(N_CTX)[None, :]).astype(jnp.float32)

    def window(inputs):
        query_w, key_w, value_w, mask_w = inputs
        dancer_mask = jnp.dot(jnp.dot(chooser, mask_w.astype(jnp.float32)), chooser.T)
        allowed = jnp.tile(dancer_mask, (FRAME_DEV, FRAME_DEV))

        def one_head(head_inputs):
            head_q, head_k, head_v = head_inputs
            scores = jnp.dot(head_q, head_k.T, preferred_element_type=jnp.float32) * 0.125
            scores = jnp.where(allowed > 0, scores, -1e+30)
            peak = lax.optimization_barrier(jnp.max(scores, axis=-1, keepdims=True))
            expo = jnp.exp(scores - peak) * allowed
            total = lax.optimization_barrier(jnp.sum(expo, axis=-1, keepdims=True))
            probs = expo.astype(jnp.bfloat16)
            mixed = jnp.dot(probs, head_v, preferred_element_type=jnp.float32)
            return mixed / total
        return lax.map(one_head, (query_w, key_w, value_w))
    attended = lax.map(window, (split_heads(queries), split_heads(keys), split_heads(values), block_mask))
    attended = attended.transpose(0, 2, 1, 3).reshape(FRAMES * DANCERS, D).astype(jnp.bfloat16)
    hidden = jnp.dot(flat, w_up, preferred_element_type=jnp.float32)
    activated = jax.nn.gelu(hidden, approximate=True).astype(jnp.bfloat16)
    branches = jnp.dot(attended, w_out, preferred_element_type=jnp.float32)
    branches = branches + jnp.dot(activated, w_down, preferred_element_type=jnp.float32)
    padded = jnp.pad(normed.astype(jnp.float32), ((2, 2), (0, 0), (0, 0)))
    convolved = jnp.zeros((FRAMES, DANCERS, D), jnp.float32)
    for offset in range(KERNEL):
        convolved = convolved + conv_weight[offset] * padded[offset:offset + FRAMES]
    total_out = tokens.astype(jnp.float32) + branches.reshape(FRAMES, DANCERS, D) + convolved
    return total_out.astype(jnp.bfloat16)
```

```python
import functools

import jax
import jax.numpy as jnp
from jax import lax
from jax.experimental import pallas as pl
from jax.experimental.pallas import tpu as pltpu
from jax.sharding import PartitionSpec as P

HEAD_DIM = 64
KERNEL = 5
MASKED = -1e30
VMEM = pltpu.CompilerParams(vmem_limit_bytes=48 * 1024 * 1024)


def from_behind(value, axis, steps):
    count = lax.axis_size(axis)
    first, last = (max(0, -steps), min(count, count - steps))
    return lax.ppermute(value, axis, [(source, source + steps) for source in range(first, last)])


def rms_norm(tokens, norm_gain):
    values = tokens.astype(jnp.float32)
    square = jnp.mean(values * values, axis=-1, keepdims=True)
    return (values * lax.rsqrt(square + 1e-05) * norm_gain).astype(jnp.bfloat16)


def across(value, axis, step):
    count = lax.axis_size(axis)
    return lax.ppermute(value, axis, [(source, source ^ step) for source in range(count)])


def convolve(normed_cols, conv_weight):
    frames_here, dancers_here, features_here = normed_cols.shape
    wide = normed_cols.astype(jnp.float32)
    before = from_behind(normed_cols[frames_here - 2 :], "tm", 1).astype(jnp.float32)
    after = from_behind(normed_cols[0:2], "tm", -1).astype(jnp.float32)
    padded = jnp.concatenate([before, wide, after], axis=0)
    convolved = jnp.zeros((frames_here, dancers_here, features_here), jnp.float32)
    for offset in range(KERNEL):
        convolved = convolved + conv_weight[offset] * padded[offset : offset + frames_here]
    return convolved


def project_kernel(n_ctx, place, *refs):
    own, firsts, seconds = refs[0], refs[1:n_ctx], refs[n_ctx : 2 * n_ctx - 1]
    near_w, far_w, farther_w = refs[2 * n_ctx - 1 : 2 * n_ctx + 2]
    outs = refs[2 * n_ctx + 2 : 3 * n_ctx + 2]
    qkv_out = refs[3 * n_ctx + 2]
    held = refs[3 * n_ctx + 3]
    tm, groups, tp = place[0], place[1], place[2]
    rows, width = own.shape
    half, near, far = rows // 2, near_w.shape[0], far_w.shape[0]
    cuts = (
        (0, near, pl.multiple_of(tm * near, near)),
        (near, far, pl.multiple_of((1 - tm) * near + groups * far, far)),
        (near + far, far, pl.multiple_of((1 - tm) * near + (1 - groups) * far, far)),
    )
    for to, size, start in cuts:
        held[0:rows, to : to + size] = own[:, pl.ds(start, size)]
        for d in range(1, n_ctx):
            here = pl.multiple_of(d * rows + tp * half, half)
            there = pl.multiple_of(d * rows + (1 - tp) * half, half)
            held[pl.ds(here, half), to : to + size] = firsts[d - 1][:, pl.ds(start, size)]
            held[pl.ds(there, half), to : to + size] = seconds[d - 1][:, pl.ds(start, size)]
    total = jnp.dot(held[:, 0:near], near_w[...], preferred_element_type=jnp.float32)
    total += jnp.dot(held[:, near : near + far], far_w[...], preferred_element_type=jnp.float32)
    total += jnp.dot(held[:, near + far :], farther_w[...], preferred_element_type=jnp.float32)
    hidden = outs[0].shape[1]
    activated = jax.nn.gelu(total[:, :hidden], approximate=True).astype(jnp.bfloat16)
    for d in range(n_ctx):
        outs[d][...] = activated[d * rows : (d + 1) * rows]
    qkv_out[...] = total[:, hidden:].astype(jnp.bfloat16)


def attend_kernel(n_ctx, place, *refs):
    masks, qkv, outs = refs[:n_ctx], refs[n_ctx], refs[n_ctx + 1 :]
    ctx = place[0]
    rows, wide = outs[0].shape
    heads = wide // HEAD_DIM
    lane_head = lax.broadcasted_iota(jnp.int32, (1, wide), 1) // HEAD_DIM
    keys = qkv[:, wide : 2 * wide]
    values = qkv[:, 2 * wide :]
    for i in range(n_ctx):
        queries = qkv[i * rows : (i + 1) * rows, 0:wide]
        bias = jnp.concatenate(
            [
                jnp.full((1, rows), jnp.where(masks[i][0, ctx ^ j] > 0, 0.0, MASKED), jnp.float32)
                for j in range(n_ctx)
            ],
            axis=1,
        )
        result = jnp.zeros((rows, wide), jnp.float32)
        for head in range(heads):
            one = jnp.where(lane_head == head, queries, jnp.zeros_like(queries))
            scores = lax.dot_general(
                one, keys, (((1,), (1,)), ((), ())), preferred_element_type=jnp.float32
            )
            scores = scores * 0.125 + bias
            peak = jnp.max(scores, axis=-1, keepdims=True)
            expo = jnp.exp(scores - peak)
            total = jnp.sum(expo, axis=-1, keepdims=True)
            mixed = jnp.dot(expo.astype(jnp.bfloat16), values, preferred_element_type=jnp.float32)
            result = jnp.where(lane_head == head, mixed / total, result)
        outs[i][...] = result.astype(jnp.bfloat16)


def join_kernel(n_ctx, place, *refs):
    ctx, tm, groups, tp = place[0], place[1], place[2], place[3]
    acts, atts = refs[:n_ctx], refs[n_ctx : 2 * n_ctx]
    near_down, near_out, far_out, base = refs[2 * n_ctx : 2 * n_ctx + 4]
    pieces = refs[2 * n_ctx + 4 : 3 * n_ctx + 4]
    keep, send = refs[3 * n_ctx + 4 : 3 * n_ctx + 6]
    act_held, att_held = refs[3 * n_ctx + 6 :]
    hidden, wide = acts[0].shape[1], atts[0].shape[1]
    for d in range(n_ctx):
        act_held[ctx ^ d] = acts[d][...]
        att_held[ctx ^ d] = atts[d][...]

    def dot(left, right):
        return jnp.dot(left, right, preferred_element_type=jnp.float32)

    near_sum = None
    far_sum = None
    for e in range(n_ctx):
        term = dot(act_held[e], near_down[e * hidden : (e + 1) * hidden])
        term += dot(att_held[e], near_out[e * wide : (e + 1) * wide])
        near_sum = term if near_sum is None else near_sum + term
        term = dot(att_held[e], far_out[e * wide : (e + 1) * wide])
        far_sum = term if far_sum is None else far_sum + term
    for step in range(n_ctx // 2):
        far_sum += dot(act_held[2 * step + groups], pieces[2 * step][...])
        far_sum += dot(act_held[2 * step + 1 - groups], pieces[2 * step + 1][...])
    same = tm == tp
    keep[...] = jnp.where(same, near_sum, far_sum) + base[...]
    send[...] = jnp.where(same, far_sum, near_sum).astype(jnp.bfloat16)


def smem():
    return pl.BlockSpec(memory_space=pltpu.SMEM)


def vmem():
    return pl.BlockSpec(memory_space=pltpu.VMEM)


def split_over_ctx(
    tokens, norm_gain, block_mask, w_query, w_key, w_value, w_out, w_up, w_down, conv_weight
):
    n_ctx = lax.axis_size("ctx")
    groups, ctx = lax.axis_index("groups"), lax.axis_index("ctx")
    tm, tp = lax.axis_index("tm"), lax.axis_index("tp")
    frames_here, dancers_here, width = tokens.shape
    rows = frames_here * dancers_here
    depth = w_query.shape[0]
    wide = w_query.shape[1] // n_ctx
    hidden = w_up.shape[1] // n_ctx
    columns = w_out.shape[1]
    packed_width = hidden + 3 * wide

    def packed(first, count):
        return jnp.concatenate(
            [
                lax.dynamic_slice(w, (first, ctx * size), (count, size))
                for w, size in ((w_up, hidden), (w_query, wide), (w_key, wide), (w_value, wide))
            ],
            axis=1,
        )

    normed_grid = rms_norm(tokens, norm_gain)
    normed = normed_grid.reshape(rows, width)
    half = lax.dynamic_slice_in_dim(normed, tp * (rows // 2), rows // 2, 0)
    firsts = [across(half, "ctx", d) for d in range(1, n_ctx)]
    masks = [block_mask[0]] + [across(block_mask[0], "ctx", d) for d in range(1, n_ctx)]
    seconds = [across(piece, "tp", 1) for piece in firsts]

    far_w = across(packed(groups * (depth // 2), depth // 2), "tm", 1)
    farther_w = across(far_w, "groups", 1)
    near_w = packed(0, depth)
    pieces = []
    for step in range(n_ctx // 2):
        start = (2 * step + groups) * hidden
        got = across(lax.dynamic_slice_in_dim(w_down, start, hidden, 0), "tm", 1)
        pieces += [got, across(got, "groups", 1)]
    far_out = across(w_out, "tm", 1)

    first_feature = tp * columns
    normed_cols = lax.dynamic_slice_in_dim(normed_grid, first_feature, columns, 2)
    token_cols = lax.dynamic_slice_in_dim(tokens, first_feature, columns, 2)
    base = (token_cols.astype(jnp.float32) + convolve(normed_cols, conv_weight)).reshape(
        rows, columns
    )

    place = jnp.stack([tm, groups, tp]).astype(jnp.int32)
    *acts, qkv = pl.pallas_call(
        functools.partial(project_kernel, n_ctx),
        out_shape=[jax.ShapeDtypeStruct((rows, hidden), jnp.bfloat16)] * n_ctx
        + [jax.ShapeDtypeStruct((n_ctx * rows, 3 * wide), jnp.bfloat16)],
        in_specs=[smem()] + [vmem()] * (2 * n_ctx + 2),
        out_specs=[vmem()] * (n_ctx + 1),
        scratch_shapes=[pltpu.VMEM((n_ctx * rows, width), jnp.bfloat16)],
        compiler_params=VMEM,
        name="project",
        cost_estimate=pl.CostEstimate(
            flops=2 * n_ctx * rows * width * packed_width,
            bytes_accessed=4 * 1024 * 1024,
            transcendentals=n_ctx * rows * hidden,
        ),
    )(place, normed, *firsts, *seconds, near_w, far_w, farther_w)
    acts = [acts[0]] + [across(acts[d], "ctx", d) for d in range(1, n_ctx)]

    place = ctx.astype(jnp.int32).reshape(1)
    atts = pl.pallas_call(
        functools.partial(attend_kernel, n_ctx),
        out_shape=[jax.ShapeDtypeStruct((rows, wide), jnp.bfloat16)] * n_ctx,
        in_specs=[smem()] * (n_ctx + 1) + [vmem()],
        out_specs=[vmem()] * n_ctx,
        compiler_params=VMEM,
        name="attend",
        cost_estimate=pl.CostEstimate(
            flops=4 * wide * (n_ctx * rows) ** 2,
            bytes_accessed=1024 * 1024,
            transcendentals=(wide // HEAD_DIM) * (n_ctx * rows) ** 2,
        ),
    )(place, *masks, qkv)
    atts = [atts[0]] + [across(atts[d], "ctx", d) for d in range(1, n_ctx)]

    place = jnp.stack([ctx, tm, groups, tp]).astype(jnp.int32)
    keep, send = pl.pallas_call(
        functools.partial(join_kernel, n_ctx),
        out_shape=[
            jax.ShapeDtypeStruct((rows, columns), jnp.float32),
            jax.ShapeDtypeStruct((rows, columns), jnp.bfloat16),
        ],
        in_specs=[smem()] + [vmem()] * (3 * n_ctx + 4),
        out_specs=[vmem()] * 2,
        scratch_shapes=[
            pltpu.VMEM((n_ctx, rows, hidden), jnp.bfloat16),
            pltpu.VMEM((n_ctx, rows, wide), jnp.bfloat16),
        ],
        compiler_params=VMEM,
        name="join",
        cost_estimate=pl.CostEstimate(
            flops=4 * rows * columns * n_ctx * (hidden + wide),
            bytes_accessed=5 * 1024 * 1024,
            transcendentals=0,
        ),
    )(place, *acts, *atts, w_down, w_out, far_out, base, *pieces)
    other = across(send, "tp", 1).astype(jnp.float32)
    return (keep + other).astype(jnp.bfloat16).reshape(frames_here, dancers_here, columns)


def gather_all(
    tokens, norm_gain, block_mask, w_query, w_key, w_value, w_out, w_up, w_down, conv_weight
):
    frames_here, dancers_here, width = tokens.shape
    rows_here = frames_here * dancers_here
    normed_grid = rms_norm(tokens, norm_gain)
    normed = normed_grid.reshape(rows_here, width)
    query_sum, key_sum, value_sum, hidden = tuple(
        jnp.dot(
            normed,
            lax.all_gather(piece, "tm", axis=0, tiled=True),
            preferred_element_type=jnp.float32,
        )
        for piece in (w_query, w_key, w_value, w_up)
    )
    local_heads = query_sum.shape[1] // HEAD_DIM
    queries = query_sum.astype(jnp.bfloat16).reshape(rows_here, local_heads, HEAD_DIM)
    grid = (frames_here, dancers_here, local_heads * HEAD_DIM)
    key_piece = lax.all_gather(
        key_sum.astype(jnp.bfloat16).reshape(grid), "ctx", axis=1, tiled=True
    )
    value_piece = lax.all_gather(
        value_sum.astype(jnp.bfloat16).reshape(grid), "ctx", axis=1, tiled=True
    )
    count = key_piece.shape[1]
    allowed = jnp.tile(jnp.repeat(block_mask[0, 0].astype(jnp.float32), dancers_here), frames_here)
    key_rows = key_piece.reshape(frames_here * count, local_heads, HEAD_DIM)
    value_rows = value_piece.reshape(frames_here * count, local_heads, HEAD_DIM)
    scores = (
        jnp.einsum("qhd,khd->hqk", queries, key_rows, preferred_element_type=jnp.float32) * 0.125
    )
    scores = jnp.where(allowed[None, None, :] > 0, scores, MASKED)
    expo = jnp.exp(scores - jnp.max(scores, axis=-1, keepdims=True)) * allowed[None, None, :]
    total = jnp.sum(expo, axis=-1)
    mixed = jnp.einsum(
        "hqk,khd->hqd", expo.astype(jnp.bfloat16), value_rows, preferred_element_type=jnp.float32
    )
    attended = (
        (mixed / total[:, :, None])
        .transpose(1, 0, 2)
        .reshape(rows_here, local_heads * HEAD_DIM)
        .astype(jnp.bfloat16)
    )
    activated = jax.nn.gelu(hidden, approximate=True).astype(jnp.bfloat16)
    out_full = lax.all_gather(w_out, "tm", axis=1, tiled=True)
    down_full = lax.all_gather(w_down, "tm", axis=1, tiled=True)
    branches = jnp.dot(attended, out_full, preferred_element_type=jnp.float32)
    branches = branches + jnp.dot(activated, down_full, preferred_element_type=jnp.float32)
    mine = lax.psum_scatter(
        branches.astype(jnp.bfloat16), "tp", scatter_dimension=1, tiled=True
    ).astype(jnp.float32)
    features_here = mine.shape[1]
    first_feature = lax.axis_index("tp") * features_here
    normed_cols = lax.dynamic_slice_in_dim(normed_grid, first_feature, features_here, 2)
    token_cols = lax.dynamic_slice_in_dim(tokens, first_feature, features_here, 2)
    result = (
        token_cols.astype(jnp.float32)
        + mine.reshape(frames_here, dancers_here, features_here)
        + convolve(normed_cols, conv_weight)
    )
    return result.astype(jnp.bfloat16)


def solution(mesh):
    n_ctx, n_tm = mesh.shape["ctx"], mesh.shape["tm"]

    def on_device(*arrays):
        local_heads = arrays[3].shape[1] // HEAD_DIM
        pairs = n_tm == 2 and mesh.shape["groups"] == 2 and mesh.shape["tp"] == 2
        even = n_ctx & (n_ctx - 1) == 0 and n_ctx > 1 and local_heads % (2 * n_ctx) == 0
        chosen = split_over_ctx if pairs and even else gather_all
        return chosen(*arrays)

    placed = (
        P(("groups", "tm"), "ctx", None),
        P(),
        P(("groups", "tm"), "ctx", None),
        P("tm", "tp"),
        P("tm", "tp"),
        P("tm", "tp"),
        P("tp", "tm"),
        P("tm", "tp"),
        P("tp", "tm"),
        P(None, "tp"),
    )
    return jax.shard_map(
        on_device,
        mesh=mesh,
        in_specs=placed,
        out_specs=P(("groups", "tm"), "ctx", "tp"),
        check_vma=False,
    )
```

```python
import functools

import jax
import jax.numpy as jnp
from jax import lax
from jax.experimental import pallas as pl
from jax.experimental.pallas import tpu as pltpu
from jax.sharding import PartitionSpec as P

HEAD_DIM = 64
KERNEL = 5
MASKED = -1e30


def from_behind(value, axis, steps):
    count = lax.axis_size(axis)
    first, last = (max(0, -steps), min(count, count - steps))
    return lax.ppermute(value, axis, [(source, source + steps) for source in range(first, last)])


def rms_norm(tokens, norm_gain):
    values = tokens.astype(jnp.float32)
    square = jnp.mean(values * values, axis=-1, keepdims=True)
    return (values * lax.rsqrt(square + 1e-05) * norm_gain).astype(jnp.bfloat16)


def across(value, axis, step):
    count = lax.axis_size(axis)
    return lax.ppermute(value, axis, [(source, source ^ step) for source in range(count)])


def two_ways(value):
    pairs = [
        (2 * source + core, 2 * (source ^ (1 + core)) + core)
        for source in range(lax.axis_size("ctx"))
        for core in range(2)
    ]
    return lax.ppermute(value, ("ctx", "tp"), pairs)


def convolve(normed_cols, conv_weight):
    frames_here, dancers_here, features_here = normed_cols.shape
    wide = normed_cols.astype(jnp.float32)
    before = from_behind(normed_cols[frames_here - 2 :], "tm", 1).astype(jnp.float32)
    after = from_behind(normed_cols[0:2], "tm", -1).astype(jnp.float32)
    padded = jnp.concatenate([before, wide, after], axis=0)
    convolved = jnp.zeros((frames_here, dancers_here, features_here), jnp.float32)
    for offset in range(KERNEL):
        convolved = convolved + conv_weight[offset] * padded[offset : offset + frames_here]
    return convolved


def begin(sems, pairs):
    copies = [
        pltpu.make_async_copy(source, target, sems.at[n]) for n, (source, target) in enumerate(pairs)
    ]
    for copy in copies:
        copy.start()
    return copies


def end(copies):
    for copy in copies:
        copy.wait()


def slot(index, size):
    return pl.ds(pl.multiple_of(index * size, size), size)


def prepare_kernel(
    n_ctx, place, tokens, gain, w_up, w_query, w_key, w_value, full, half, first, second, sems
):
    ctx, tm, groups, tp = place[0], place[1], place[2], place[3]
    rows = tokens.shape[0]
    count = first.shape[0]
    edge = second.shape[0] - count
    pairs, column = [], 0
    for w in (w_up, w_query, w_key, w_value):
        size = w.shape[1] // n_ctx
        for step, out in enumerate((first, second)):
            source = w.at[slot(2 * groups + step, count), slot(ctx, size)]
            pairs.append((source, out.at[0:count, column : column + size]))
        column += size
    copies = begin(sems, pairs)
    values = tokens[...].astype(jnp.float32)
    square = jnp.mean(values * values, axis=-1, keepdims=True)
    full[...] = (values * lax.rsqrt(square + 1e-05) * gain[...]).astype(jnp.bfloat16)
    half[...] = full[slot(tp, rows // 2), :]
    columns = full.shape[1] // 2
    last_edge = full[rows - edge :, slot(tp, columns)]
    first_edge = full[0:edge, slot(tp, columns)]
    second[count:, 0:columns] = jnp.where(tm == 0, last_edge, first_edge)
    second[count:, columns:] = jnp.zeros((edge, second.shape[1] - columns), jnp.bfloat16)
    end(copies)


def convolve_kernel(per_frame, place, tokens, full, halo, taps, base, held):
    tm, tp = place[1], place[3]
    rows, columns = base.shape
    edge = 16
    margin = 2 * per_frame
    near = halo[halo.shape[0] - edge :, 0:columns].astype(jnp.float32)
    zeros = jnp.zeros((edge, columns), jnp.float32)
    held[0:edge, :] = jnp.where(tm == 1, near, zeros)
    held[edge : edge + rows, :] = full[:, slot(tp, columns)].astype(jnp.float32)
    held[edge + rows :, :] = jnp.where(tm == 0, near, zeros)
    total = tokens[:, slot(tp, columns)].astype(jnp.float32)
    for offset in range(KERNEL):
        start = edge - margin + offset * per_frame
        total += taps[offset : offset + 1, :] * held[start : start + rows, :]
    base[...] = total


def project_kernel(n_ctx, place, *refs):
    own, block, other_block, piece, other_piece = refs[:5]
    w_up, w_query, w_key, w_value, first, second, far_first, far_second = refs[5:13]
    acts, qkv = refs[13 : 13 + n_ctx], refs[13 + n_ctx]
    held, weights, sems = refs[14 + n_ctx :]
    ctx, tm, groups, tp = place[0], place[1], place[2], place[3]
    rows, count = own.shape[0], first.shape[0]
    pairs, column = [], 0
    for w in (w_up, w_query, w_key, w_value):
        size = w.shape[1] // n_ctx
        target = weights.at[slot(tm, w.shape[0]), column : column + size]
        pairs.append((w.at[:, slot(ctx, size)], target))
        column += size
    quarters = 4 * (1 - tm) + 2 * groups, 4 * (1 - tm) + 2 * (1 - groups)
    pairs += [
        (first, weights.at[slot(quarters[0], count)]),
        (second.at[0:count], weights.at[slot(quarters[0] + 1, count)]),
        (far_first, weights.at[slot(quarters[1], count)]),
        (far_second.at[0:count], weights.at[slot(quarters[1] + 1, count)]),
        (own, held.at[0:rows]),
        (block, held.at[slot(1 + tp, rows)]),
        (other_block, held.at[slot(2 - tp, rows)]),
        (piece, held.at[slot(6 + tp, rows // 2)]),
        (other_piece, held.at[slot(7 - tp, rows // 2)]),
    ]
    end(begin(sems, pairs))
    total = jnp.dot(held[...], weights[...], preferred_element_type=jnp.float32)
    hidden = acts[0].shape[1]
    activated = jax.nn.gelu(total[:, :hidden], approximate=True).astype(jnp.bfloat16)
    for d in range(n_ctx):
        acts[d][...] = activated[d * rows : (d + 1) * rows]
    qkv[...] = total[:, hidden:].astype(jnp.bfloat16)


def attend_kernel(n_ctx, i, place, mask, activated, qkv, out):
    ctx = place[0]
    rows, hidden = activated.shape
    wide = out.shape[1] - hidden
    lane_head = lax.broadcasted_iota(jnp.int32, (1, wide), 1) // HEAD_DIM
    queries = qkv[i * rows : (i + 1) * rows, 0:wide]
    keys = qkv[:, wide : 2 * wide]
    values = qkv[:, 2 * wide :]
    bias = jnp.concatenate(
        [
            jnp.full((1, rows), jnp.where(mask[0, ctx ^ j] > 0, 0.0, MASKED), jnp.float32)
            for j in range(n_ctx)
        ],
        axis=1,
    )
    result = jnp.zeros((rows, wide), jnp.float32)
    for head in range(wide // HEAD_DIM):
        one = jnp.where(lane_head == head, queries, jnp.zeros_like(queries))
        scores = lax.dot_general(
            one, keys, (((1,), (1,)), ((), ())), preferred_element_type=jnp.float32
        )
        scores = scores * 0.125 + bias
        peak = jnp.max(scores, axis=-1, keepdims=True)
        expo = jnp.exp(scores - peak)
        total = jnp.sum(expo, axis=-1, keepdims=True)
        mixed = jnp.dot(expo.astype(jnp.bfloat16), values, preferred_element_type=jnp.float32)
        result = jnp.where(lane_head == head, mixed / total, result)
    out[:, 0:hidden] = activated[...]
    out[:, hidden:] = result.astype(jnp.bfloat16)


def join_kernel(n_ctx, place, *refs):
    near_down, near_out, base = refs[:3]
    far_down, farther_down, far_out = refs[3:6]
    parts = refs[6 : 6 + n_ctx]
    keep, send, down, out, acts, atts, sems = refs[6 + n_ctx :]
    ctx, tm, groups, tp = place[0], place[1], place[2], place[3]
    hidden, wide = acts.shape[1] // n_ctx, atts.shape[1] // n_ctx
    count = far_down.shape[0]
    pairs = []
    for d in range(n_ctx):
        pairs.append((parts[d].at[:, 0:hidden], acts.at[:, slot(ctx ^ d, hidden)]))
        pairs.append((parts[d].at[:, hidden:], atts.at[:, slot(ctx ^ d, wide)]))
    pairs.append((far_out, out))
    pairs.append((far_down, down.at[slot(groups, count)]))
    pairs.append((farther_down, down.at[slot(1 - groups, count)]))
    copies = begin(sems, pairs)

    def dot(left, right):
        return jnp.dot(left[...], right[...], preferred_element_type=jnp.float32)

    end(copies[: 2 * n_ctx])
    near_sum = dot(acts, near_down) + dot(atts, near_out)
    end(copies[2 * n_ctx :])
    far_sum = dot(acts, down) + dot(atts, out)
    same = tm == tp
    keep[...] = jnp.where(same, near_sum, far_sum) + base[...]
    send[...] = jnp.where(same, far_sum, near_sum).astype(jnp.bfloat16)


SMEM = pl.BlockSpec(memory_space=pltpu.SMEM)
VMEM = pl.BlockSpec(memory_space=pltpu.VMEM)
ANY = pl.BlockSpec(memory_space=pl.ANY)


def call(kernel, name, outs, ins, scratch=(), flops=0, moved=1 << 20, transcendentals=0):
    specs, values = zip(*ins)
    return pl.pallas_call(
        kernel,
        out_shape=[jax.ShapeDtypeStruct(shape, dtype) for shape, dtype in outs],
        in_specs=list(specs),
        out_specs=[VMEM] * len(outs),
        scratch_shapes=list(scratch),
        compiler_params=pltpu.CompilerParams(vmem_limit_bytes=32 * 1024 * 1024),
        name=name,
        cost_estimate=pl.CostEstimate(
            flops=flops, bytes_accessed=moved, transcendentals=transcendentals
        ),
    )(*values)


def split_over_ctx(
    tokens, norm_gain, block_mask, w_query, w_key, w_value, w_out, w_up, w_down, conv_weight
):
    n_ctx = lax.axis_size("ctx")
    groups, ctx = lax.axis_index("groups"), lax.axis_index("ctx")
    tm, tp = lax.axis_index("tm"), lax.axis_index("tp")
    frames_here, dancers_here, width = tokens.shape
    rows = frames_here * dancers_here
    depth = w_query.shape[0]
    wide = w_query.shape[1] // n_ctx
    hidden = w_up.shape[1] // n_ctx
    columns = w_out.shape[1]
    packed = hidden + 3 * wide
    bf16, f32 = jnp.bfloat16, jnp.float32
    place = jnp.stack([ctx, tm, groups, tp]).astype(jnp.int32)
    token_rows = tokens.reshape(rows, width)
    quarter = depth // 4

    full, half, first, second = call(
        functools.partial(prepare_kernel, n_ctx),
        "prepare",
        [
            ((rows, width), bf16),
            ((rows // 2, width), bf16),
            ((quarter, packed), bf16),
            ((quarter + 16, packed), bf16),
        ],
        [(SMEM, place), (VMEM, token_rows), (VMEM, norm_gain.reshape(1, width))]
        + [(ANY, w) for w in (w_up, w_query, w_key, w_value)],
        [pltpu.SemaphoreType.DMA((8,))],
    )
    block = two_ways(full)
    piece = across(half, "ctx", 3)
    x_first = across(first, "tm", 1)
    x_second = across(second, "tm", 1)
    y_first = across(x_first, "groups", 1)
    y_second = across(x_second, "groups", 1)
    masks = [block_mask[0]] + [across(block_mask[0], "ctx", d) for d in range(1, n_ctx)]
    other_block = across(block, "tp", 1)
    other_piece = across(piece, "tp", 1)
    half_down = w_down.shape[0] // 2
    x_down = across(lax.dynamic_slice_in_dim(w_down, groups * half_down, half_down, 0), "tm", 1)
    y_down = across(x_down, "groups", 1)
    x_out = across(w_out, "tm", 1)

    (base,) = call(
        functools.partial(convolve_kernel, dancers_here),
        "convolve",
        [((rows, columns), f32)],
        [
            (SMEM, place),
            (VMEM, token_rows),
            (VMEM, full),
            (VMEM, x_second),
            (VMEM, conv_weight),
        ],
        [pltpu.VMEM((rows + 32, columns), f32)],
    )
    *acts, qkv = call(
        functools.partial(project_kernel, n_ctx),
        "project",
        [((rows, hidden), bf16)] * n_ctx + [((n_ctx * rows, 3 * wide), bf16)],
        [(SMEM, place)]
        + [(ANY, value) for value in (full, block, other_block, piece, other_piece)]
        + [(ANY, value) for value in (w_up, w_query, w_key, w_value)]
        + [(ANY, value) for value in (x_first, x_second, y_first, y_second)],
        [
            pltpu.VMEM((n_ctx * rows, width), bf16),
            pltpu.VMEM((width, packed), bf16),
            pltpu.SemaphoreType.DMA((13,)),
        ],
        flops=2 * n_ctx * rows * width * packed,
        moved=4 << 20,
        transcendentals=n_ctx * rows * hidden,
    )
    parts = [None] * n_ctx
    for i in (2, 3, 1, 0):
        (part,) = call(
            functools.partial(attend_kernel, n_ctx, i),
            "attend",
            [((rows, hidden + wide), bf16)],
            [(SMEM, place), (SMEM, masks[i]), (VMEM, acts[i]), (VMEM, qkv)],
            flops=4 * wide * n_ctx * rows * rows,
            transcendentals=(wide // HEAD_DIM) * n_ctx * rows * rows,
        )
        parts[i] = across(part, "ctx", i) if i else part
    keep, send = call(
        functools.partial(join_kernel, n_ctx),
        "join",
        [((rows, columns), f32), ((rows, columns), bf16)],
        [(SMEM, place), (VMEM, w_down), (VMEM, w_out), (VMEM, base)]
        + [(ANY, value) for value in (x_down, y_down, x_out)]
        + [(ANY, value) for value in parts],
        [
            pltpu.VMEM(w_down.shape, bf16),
            pltpu.VMEM(w_out.shape, bf16),
            pltpu.VMEM((rows, w_down.shape[0]), bf16),
            pltpu.VMEM((rows, w_out.shape[0]), bf16),
            pltpu.SemaphoreType.DMA((2 * n_ctx + 3,)),
        ],
        flops=4 * rows * columns * n_ctx * (hidden + wide),
        moved=4 << 20,
    )
    other = across(send, "tp", 1).astype(f32)
    return (keep + other).astype(bf16).reshape(frames_here, dancers_here, columns)


def gather_all(
    tokens, norm_gain, block_mask, w_query, w_key, w_value, w_out, w_up, w_down, conv_weight
):
    frames_here, dancers_here, width = tokens.shape
    rows_here = frames_here * dancers_here
    normed_grid = rms_norm(tokens, norm_gain)
    normed = normed_grid.reshape(rows_here, width)
    query_sum, key_sum, value_sum, hidden = tuple(
        jnp.dot(
            normed,
            lax.all_gather(piece, "tm", axis=0, tiled=True),
            preferred_element_type=jnp.float32,
        )
        for piece in (w_query, w_key, w_value, w_up)
    )
    local_heads = query_sum.shape[1] // HEAD_DIM
    queries = query_sum.astype(jnp.bfloat16).reshape(rows_here, local_heads, HEAD_DIM)
    grid = (frames_here, dancers_here, local_heads * HEAD_DIM)
    key_piece = lax.all_gather(
        key_sum.astype(jnp.bfloat16).reshape(grid), "ctx", axis=1, tiled=True
    )
    value_piece = lax.all_gather(
        value_sum.astype(jnp.bfloat16).reshape(grid), "ctx", axis=1, tiled=True
    )
    count = key_piece.shape[1]
    allowed = jnp.tile(jnp.repeat(block_mask[0, 0].astype(jnp.float32), dancers_here), frames_here)
    key_rows = key_piece.reshape(frames_here * count, local_heads, HEAD_DIM)
    value_rows = value_piece.reshape(frames_here * count, local_heads, HEAD_DIM)
    scores = (
        jnp.einsum("qhd,khd->hqk", queries, key_rows, preferred_element_type=jnp.float32) * 0.125
    )
    scores = jnp.where(allowed[None, None, :] > 0, scores, MASKED)
    expo = jnp.exp(scores - jnp.max(scores, axis=-1, keepdims=True)) * allowed[None, None, :]
    total = jnp.sum(expo, axis=-1)
    mixed = jnp.einsum(
        "hqk,khd->hqd", expo.astype(jnp.bfloat16), value_rows, preferred_element_type=jnp.float32
    )
    attended = (
        (mixed / total[:, :, None])
        .transpose(1, 0, 2)
        .reshape(rows_here, local_heads * HEAD_DIM)
        .astype(jnp.bfloat16)
    )
    activated = jax.nn.gelu(hidden, approximate=True).astype(jnp.bfloat16)
    out_full = lax.all_gather(w_out, "tm", axis=1, tiled=True)
    down_full = lax.all_gather(w_down, "tm", axis=1, tiled=True)
    branches = jnp.dot(attended, out_full, preferred_element_type=jnp.float32)
    branches = branches + jnp.dot(activated, down_full, preferred_element_type=jnp.float32)
    mine = lax.psum_scatter(
        branches.astype(jnp.bfloat16), "tp", scatter_dimension=1, tiled=True
    ).astype(jnp.float32)
    features_here = mine.shape[1]
    first_feature = lax.axis_index("tp") * features_here
    normed_cols = lax.dynamic_slice_in_dim(normed_grid, first_feature, features_here, 2)
    token_cols = lax.dynamic_slice_in_dim(tokens, first_feature, features_here, 2)
    result = (
        token_cols.astype(jnp.float32)
        + mine.reshape(frames_here, dancers_here, features_here)
        + convolve(normed_cols, conv_weight)
    )
    return result.astype(jnp.bfloat16)


def solution(mesh):
    n_ctx, n_tm = mesh.shape["ctx"], mesh.shape["tm"]

    def on_device(*arrays):
        local_heads = arrays[3].shape[1] // HEAD_DIM
        pairs = n_tm == 2 and mesh.shape["groups"] == 2 and mesh.shape["tp"] == 2
        even = n_ctx == 4 and local_heads % (2 * n_ctx) == 0
        chosen = split_over_ctx if pairs and even else gather_all
        return chosen(*arrays)

    placed = (
        P(("groups", "tm"), "ctx", None),
        P(),
        P(("groups", "tm"), "ctx", None),
        P("tm", "tp"),
        P("tm", "tp"),
        P("tm", "tp"),
        P("tp", "tm"),
        P("tm", "tp"),
        P("tp", "tm"),
        P(None, "tp"),
    )
    return jax.shard_map(
        on_device,
        mesh=mesh,
        in_specs=placed,
        out_specs=P(("groups", "tm"), "ctx", "tp"),
        check_vma=False,
    )
```

```python
import functools

import jax
import jax.numpy as jnp
from jax import lax
from jax.experimental import pallas as pl
from jax.experimental.pallas import tpu as pltpu
from jax.sharding import PartitionSpec as P

HEAD_DIM = 64
KERNEL = 5
MASKED = -1e30
LANES = 128
AXES = ("ctx", "tm", "groups", "tp")


def from_behind(value, axis, steps):
    count = lax.axis_size(axis)
    first, last = (max(0, -steps), min(count, count - steps))
    return lax.ppermute(value, axis, [(source, source + steps) for source in range(first, last)])


def rms_norm(tokens, norm_gain):
    values = tokens.astype(jnp.float32)
    square = jnp.mean(values * values, axis=-1, keepdims=True)
    return (values * lax.rsqrt(square + 1e-05) * norm_gain).astype(jnp.bfloat16)


def across(value, axis, step):
    count = lax.axis_size(axis)
    return lax.ppermute(value, axis, [(source, source ^ step) for source in range(count)])


def two_ways(value, steps):
    pairs = [
        (2 * source + core, 2 * (source ^ steps[core]) + core)
        for source in range(lax.axis_size("ctx"))
        for core in range(2)
    ]
    return lax.ppermute(value, ("ctx", "tp"), pairs)


def convolve(normed_cols, conv_weight):
    frames_here, dancers_here, features_here = normed_cols.shape
    wide = normed_cols.astype(jnp.float32)
    before = from_behind(normed_cols[frames_here - 2 :], "tm", 1).astype(jnp.float32)
    after = from_behind(normed_cols[0:2], "tm", -1).astype(jnp.float32)
    padded = jnp.concatenate([before, wide, after], axis=0)
    convolved = jnp.zeros((frames_here, dancers_here, features_here), jnp.float32)
    for offset in range(KERNEL):
        convolved = convolved + conv_weight[offset] * padded[offset : offset + frames_here]
    return convolved


def begin(sems, pairs):
    copies = [
        pltpu.make_async_copy(source, target, sems.at[n]) for n, (source, target) in enumerate(pairs)
    ]
    for copy in copies:
        copy.start()
    return copies


def end(copies):
    for copy in copies:
        copy.wait()


def slot(index, size):
    return pl.ds(pl.multiple_of(index * size, size), size)


def prepare_kernel(
    n_ctx, mask, tokens, gain, w_up, w_query, w_key, w_value, full, first, second, sems
):
    ctx, tm, groups, tp = (lax.axis_index(name) for name in AXES)
    count = first.shape[0]
    pairs = []
    for step, out in enumerate((first, second)):
        column = 0
        for w in (w_up, w_query, w_key, w_value):
            size = w.shape[1] // n_ctx
            source = w.at[slot(2 * groups + step, count), slot(ctx, size)]
            pairs.append((source, out.at[0:count, column : column + size]))
            column += size
    copies = begin(sems, pairs)
    rows, width = tokens.shape
    values = tokens[...].astype(jnp.float32)
    square = jnp.mean(values * values, axis=-1, keepdims=True)
    full[0:rows, :] = (values * lax.rsqrt(square + 1e-05) * gain[...]).astype(jnp.bfloat16)
    entries = [
        jnp.full((8, LANES), mask[0, e].astype(jnp.float32), jnp.float32) for e in range(n_ctx)
    ]
    entries.append(jnp.zeros((8, width - n_ctx * LANES), jnp.float32))
    full[rows:, :] = jnp.concatenate(entries, axis=1).astype(jnp.bfloat16)
    edge = second.shape[0] - count
    columns = width // 2
    last_edge = full[rows - edge : rows, slot(tp, columns)]
    first_edge = full[0:edge, slot(tp, columns)]
    second[count:, 0:columns] = jnp.where(tm == 0, last_edge, first_edge)
    second[count:, columns:] = jnp.zeros((edge, second.shape[1] - columns), jnp.bfloat16)
    end(copies)


def pack_near_kernel(n_ctx, after, w_up, w_query, w_key, w_value, near, sems):
    ctx = lax.axis_index("ctx")
    pairs, column = [], 0
    for w in (w_up, w_query, w_key, w_value):
        size = w.shape[1] // n_ctx
        pairs.append((w.at[:, slot(ctx, size)], near.at[:, column : column + size]))
        column += size
    end(begin(sems, pairs))


def convolve_kernel(per_frame, tokens, full, halo, taps, base, held):
    tm, tp = lax.axis_index("tm"), lax.axis_index("tp")
    rows, columns = base.shape
    edge = 16
    margin = 2 * per_frame
    near = halo[halo.shape[0] - edge :, 0:columns].astype(jnp.float32)
    zeros = jnp.zeros((edge, columns), jnp.float32)
    held[0:edge, :] = jnp.where(tm == 1, near, zeros)
    held[edge : edge + rows, :] = full[0:rows, slot(tp, columns)].astype(jnp.float32)
    held[edge + rows :, :] = jnp.where(tm == 0, near, zeros)
    total = tokens[:, slot(tp, columns)].astype(jnp.float32)
    for offset in range(KERNEL):
        start = edge - margin + offset * per_frame
        total += taps[offset : offset + 1, :] * held[start : start + rows, :]
    base[...] = total


def project_kernel(n_ctx, *refs):
    own, block, other_block, piece, other_piece = refs[:5]
    near, first, second, far_first, far_second = refs[5:10]
    acts = refs[10 : 10 + n_ctx]
    queries, keys, values, bias, held, far = refs[10 + n_ctx :]
    ctx, tm, groups, tp = (lax.axis_index(name) for name in AXES)
    rows, count, depth = own.shape[0] - 8, first.shape[0], near.shape[0]
    sources = (
        (own, slot(0, rows), rows),
        (block, slot(1 + tp, rows), rows),
        (other_block, slot(2 - tp, rows), rows),
        (piece, slot(6 + tp, rows // 2), rows // 2),
        (other_piece, slot(7 - tp, rows // 2), rows // 2),
    )
    half = depth // 2
    cuts = ((0, slot(tm, depth), depth), (depth, slot(2 * (1 - tm) + groups, half), half))
    cuts += ((depth + half, slot(2 * (1 - tm) + 1 - groups, half), half),)
    for source, target, size in sources:
        for to, lanes, wide in cuts:
            held[target, to : to + wide] = source[0:size, lanes]
    far[0:count, :] = first[...]
    far[count : 2 * count, :] = second[0:count, :]
    far[2 * count : 3 * count, :] = far_first[...]
    far[3 * count :, :] = far_second[0:count, :]
    total = jnp.dot(held[:, 0:depth], near[...], preferred_element_type=jnp.float32)
    total += jnp.dot(held[:, depth:], far[...], preferred_element_type=jnp.float32)
    hidden, wide = acts[0].shape[1], queries.shape[1]
    activated = jax.nn.gelu(total[:, :hidden], approximate=True).astype(jnp.bfloat16)
    for d in range(n_ctx):
        acts[d][...] = activated[d * rows : (d + 1) * rows]
    projected = total[:, hidden:].astype(jnp.bfloat16)
    queries[...] = projected[:, 0:wide]
    keys[...] = projected[:, wide : 2 * wide]
    values[...] = projected[:, 2 * wide :].T
    for j in range(n_ctx):
        lanes = slot(ctx ^ j, LANES)
        one, other = block[rows:, lanes], other_block[rows:, lanes]
        last, other_last = piece[rows // 2 :, lanes], other_piece[rows // 2 :, lanes]
        entries = (
            own[rows:, lanes],
            jnp.where(tp == 0, one, other),
            jnp.where(tp == 0, other, one),
            jnp.where(tp == 0, other_last, last),
        )
        for i, entry in enumerate(entries):
            flag = entry.astype(jnp.float32)
            target = slice(j * LANES, (j + 1) * LANES)
            bias[8 * i : 8 * (i + 1), target] = jnp.where(flag > 0, 0.0, MASKED)


def attend_kernel(n_ctx, i, activated, queries, keys, values, bias, out):
    rows, hidden = activated.shape
    wide = out.shape[1] - hidden
    block = queries[i * rows : (i + 1) * rows, :]
    lane_head = lax.broadcasted_iota(jnp.int32, (1, wide), 1) // HEAD_DIM
    allowed = jnp.concatenate(
        [
            jnp.broadcast_to(bias[8 * i : 8 * i + 1, j * LANES : (j + 1) * LANES], (rows, rows))
            for j in range(n_ctx)
        ],
        axis=0,
    )
    results = []
    for head in range(wide // HEAD_DIM):
        one = jnp.where(lane_head == head, block, jnp.zeros_like(block))
        scores = lax.dot_general(
            keys[...], one, (((1,), (1,)), ((), ())), preferred_element_type=jnp.float32
        )
        scores = scores * 0.125 + allowed
        peak = jnp.max(scores, axis=0, keepdims=True)
        expo = jnp.exp(scores - peak)
        total = jnp.sum(expo, axis=0, keepdims=True)
        mixed = jnp.dot(
            values[head * HEAD_DIM : (head + 1) * HEAD_DIM, :],
            expo.astype(jnp.bfloat16),
            preferred_element_type=jnp.float32,
        )
        results.append(mixed / total)
    out[:, 0:hidden] = activated[...]
    out[:, hidden:] = jnp.concatenate(results, axis=0).T.astype(jnp.bfloat16)


def join_kernel(n_ctx, *refs):
    near_down, near_out, base = refs[:3]
    far_down, farther_down, far_out = refs[3:6]
    parts = refs[6 : 6 + n_ctx]
    keep, send, down, out, acts, atts, sems = refs[6 + n_ctx :]
    ctx, tm, groups, tp = (lax.axis_index(name) for name in AXES)
    hidden, wide = acts.shape[1] // n_ctx, atts.shape[1] // n_ctx
    count = far_down.shape[0]
    pairs = []
    for d in range(n_ctx):
        pairs.append((parts[d].at[:, 0:hidden], acts.at[:, slot(ctx ^ d, hidden)]))
        pairs.append((parts[d].at[:, hidden:], atts.at[:, slot(ctx ^ d, wide)]))
    pairs.append((far_out, out))
    pairs.append((far_down, down.at[slot(groups, count)]))
    pairs.append((farther_down, down.at[slot(1 - groups, count)]))
    copies = begin(sems, pairs)

    def dot(left, right):
        return jnp.dot(left[...], right[...], preferred_element_type=jnp.float32)

    end(copies[: 2 * n_ctx])
    near_sum = dot(acts, near_down) + dot(atts, near_out)
    end(copies[2 * n_ctx :])
    far_sum = dot(acts, down) + dot(atts, out)
    same = tm == tp
    keep[...] = jnp.where(same, near_sum, far_sum) + base[...]
    send[...] = jnp.where(same, far_sum, near_sum).astype(jnp.bfloat16)


SMEM = pl.BlockSpec(memory_space=pltpu.SMEM)
VMEM = pl.BlockSpec(memory_space=pltpu.VMEM)
ANY = pl.BlockSpec(memory_space=pl.ANY)


def call(
    kernel, name, outs, ins, scratch=(), flops=0, moved=1 << 20, transcendentals=0, limit=16 << 20
):
    specs, values = zip(*ins)
    return pl.pallas_call(
        kernel,
        out_shape=[jax.ShapeDtypeStruct(shape, dtype) for shape, dtype in outs],
        in_specs=list(specs),
        out_specs=[VMEM] * len(outs),
        scratch_shapes=list(scratch),
        compiler_params=pltpu.CompilerParams(vmem_limit_bytes=limit),
        name=name,
        cost_estimate=pl.CostEstimate(
            flops=flops, bytes_accessed=moved, transcendentals=transcendentals
        ),
    )(*values)


def split_over_ctx(
    tokens, norm_gain, block_mask, w_query, w_key, w_value, w_out, w_up, w_down, conv_weight
):
    n_ctx = lax.axis_size("ctx")
    groups, ctx = lax.axis_index("groups"), lax.axis_index("ctx")
    tm, tp = lax.axis_index("tm"), lax.axis_index("tp")
    frames_here, dancers_here, width = tokens.shape
    rows = frames_here * dancers_here
    depth = w_query.shape[0]
    wide = w_query.shape[1] // n_ctx
    hidden = w_up.shape[1] // n_ctx
    columns = w_out.shape[1]
    packed = hidden + 3 * wide
    bf16, f32 = jnp.bfloat16, jnp.float32
    token_rows = tokens.reshape(rows, width)
    quarter = depth // 4

    full, first, second = call(
        functools.partial(prepare_kernel, n_ctx),
        "prepare",
        [
            ((rows + 8, width), bf16),
            ((quarter, packed), bf16),
            ((quarter + 16, packed), bf16),
        ],
        [
            (SMEM, block_mask[0]),
            (VMEM, token_rows),
            (VMEM, norm_gain.reshape(1, width)),
        ]
        + [(ANY, w) for w in (w_up, w_query, w_key, w_value)],
        [pltpu.SemaphoreType.DMA((8,))],
        limit=None,
    )
    (near,) = call(
        functools.partial(pack_near_kernel, n_ctx),
        "pack_near",
        [((depth, packed), bf16)],
        [(ANY, w) for w in (second, w_up, w_query, w_key, w_value)],
        [pltpu.SemaphoreType.DMA((4,))],
    )
    block = two_ways(full, (1, 2))
    piece = lax.dynamic_slice_in_dim(block, tp * (rows // 2), rows // 2 + 8, 0)
    piece = two_ways(piece, (2, 1))
    x_first = across(first, "tm", 1)
    x_second = across(second, "tm", 1)
    y_first = across(x_first, "groups", 1)
    y_second = across(x_second, "groups", 1)
    other_block = across(block, "tp", 1)
    other_piece = across(piece, "tp", 1)
    half_down = w_down.shape[0] // 2
    sent_down = lax.dynamic_slice_in_dim(w_down, groups * half_down, half_down, 0)
    sent_down, sent_out, _ = lax.optimization_barrier(
        (sent_down, w_out, (second,))
    )
    x_down = across(sent_down, "tm", 1)
    x_out = across(sent_out, "tm", 1)

    (base,) = call(
        functools.partial(convolve_kernel, dancers_here),
        "convolve",
        [((rows, columns), f32)],
        [
            (VMEM, token_rows),
            (VMEM, full),
            (VMEM, x_second),
            (VMEM, conv_weight),
        ],
        [pltpu.VMEM((rows + 32, columns), f32)],
    )
    *acts, queries, keys, values, bias = call(
        functools.partial(project_kernel, n_ctx),
        "project",
        [((rows, hidden), bf16)] * n_ctx
        + [((n_ctx * rows, wide), bf16)] * 2
        + [((wide, n_ctx * rows), bf16), ((8 * n_ctx, n_ctx * LANES), f32)],
        [(VMEM, value) for value in (full, block, other_block, piece, other_piece)]
        + [(VMEM, value) for value in (near, x_first, x_second, y_first, y_second)],
        [
            pltpu.VMEM((n_ctx * rows, width), bf16),
            pltpu.VMEM((depth, packed), bf16),
        ],
        flops=8 * n_ctx * rows * width * packed,
        moved=64 << 20,
        transcendentals=n_ctx * rows * hidden,
    )
    parts = [None] * n_ctx
    for i in (2, 3, 1, 0):
        (part,) = call(
            functools.partial(attend_kernel, n_ctx, i),
            "attend",
            [((rows, hidden + wide), bf16)],
            [(VMEM, value) for value in (acts[i], queries, keys, values, bias)],
            flops=4 * wide * n_ctx * rows * rows,
            transcendentals=(wide // HEAD_DIM) * n_ctx * rows * rows,
        )
        if i == 1:
            x_down, part = lax.optimization_barrier((x_down, part))
        parts[i] = across(part, "ctx", i) if i else part
    y_down = across(x_down, "groups", 1)
    keep, send = call(
        functools.partial(join_kernel, n_ctx),
        "join",
        [((rows, columns), f32), ((rows, columns), bf16)],
        [(VMEM, w_down), (VMEM, w_out), (VMEM, base)]
        + [(ANY, value) for value in (x_down, y_down, x_out)]
        + [(ANY, value) for value in parts],
        [
            pltpu.VMEM(w_down.shape, bf16),
            pltpu.VMEM(w_out.shape, bf16),
            pltpu.VMEM((rows, w_down.shape[0]), bf16),
            pltpu.VMEM((rows, w_out.shape[0]), bf16),
            pltpu.SemaphoreType.DMA((2 * n_ctx + 3,)),
        ],
        flops=4 * rows * columns * n_ctx * (hidden + wide),
        moved=4 << 20,
    )
    other = across(send, "tp", 1).astype(f32)
    return (keep + other).astype(bf16).reshape(frames_here, dancers_here, columns)


def gather_all(
    tokens, norm_gain, block_mask, w_query, w_key, w_value, w_out, w_up, w_down, conv_weight
):
    frames_here, dancers_here, width = tokens.shape
    rows_here = frames_here * dancers_here
    normed_grid = rms_norm(tokens, norm_gain)
    normed = normed_grid.reshape(rows_here, width)
    query_sum, key_sum, value_sum, hidden = tuple(
        jnp.dot(
            normed,
            lax.all_gather(piece, "tm", axis=0, tiled=True),
            preferred_element_type=jnp.float32,
        )
        for piece in (w_query, w_key, w_value, w_up)
    )
    local_heads = query_sum.shape[1] // HEAD_DIM
    queries = query_sum.astype(jnp.bfloat16).reshape(rows_here, local_heads, HEAD_DIM)
    grid = (frames_here, dancers_here, local_heads * HEAD_DIM)
    key_piece = lax.all_gather(
        key_sum.astype(jnp.bfloat16).reshape(grid), "ctx", axis=1, tiled=True
    )
    value_piece = lax.all_gather(
        value_sum.astype(jnp.bfloat16).reshape(grid), "ctx", axis=1, tiled=True
    )
    count = key_piece.shape[1]
    allowed = jnp.tile(jnp.repeat(block_mask[0, 0].astype(jnp.float32), dancers_here), frames_here)
    key_rows = key_piece.reshape(frames_here * count, local_heads, HEAD_DIM)
    value_rows = value_piece.reshape(frames_here * count, local_heads, HEAD_DIM)
    scores = (
        jnp.einsum("qhd,khd->hqk", queries, key_rows, preferred_element_type=jnp.float32) * 0.125
    )
    scores = jnp.where(allowed[None, None, :] > 0, scores, MASKED)
    expo = jnp.exp(scores - jnp.max(scores, axis=-1, keepdims=True)) * allowed[None, None, :]
    total = jnp.sum(expo, axis=-1)
    mixed = jnp.einsum(
        "hqk,khd->hqd", expo.astype(jnp.bfloat16), value_rows, preferred_element_type=jnp.float32
    )
    attended = (
        (mixed / total[:, :, None])
        .transpose(1, 0, 2)
        .reshape(rows_here, local_heads * HEAD_DIM)
        .astype(jnp.bfloat16)
    )
    activated = jax.nn.gelu(hidden, approximate=True).astype(jnp.bfloat16)
    out_full = lax.all_gather(w_out, "tm", axis=1, tiled=True)
    down_full = lax.all_gather(w_down, "tm", axis=1, tiled=True)
    branches = jnp.dot(attended, out_full, preferred_element_type=jnp.float32)
    branches = branches + jnp.dot(activated, down_full, preferred_element_type=jnp.float32)
    mine = lax.psum_scatter(
        branches.astype(jnp.bfloat16), "tp", scatter_dimension=1, tiled=True
    ).astype(jnp.float32)
    features_here = mine.shape[1]
    first_feature = lax.axis_index("tp") * features_here
    normed_cols = lax.dynamic_slice_in_dim(normed_grid, first_feature, features_here, 2)
    token_cols = lax.dynamic_slice_in_dim(tokens, first_feature, features_here, 2)
    result = (
        token_cols.astype(jnp.float32)
        + mine.reshape(frames_here, dancers_here, features_here)
        + convolve(normed_cols, conv_weight)
    )
    return result.astype(jnp.bfloat16)


def solution(mesh):
    n_ctx, n_tm = mesh.shape["ctx"], mesh.shape["tm"]

    def on_device(*arrays):
        local_heads = arrays[3].shape[1] // HEAD_DIM
        pairs = n_tm == 2 and mesh.shape["groups"] == 2 and mesh.shape["tp"] == 2
        even = n_ctx == 4 and local_heads == 2 * n_ctx
        chosen = split_over_ctx if pairs and even else gather_all
        return chosen(*arrays)

    placed = (
        P(("groups", "tm"), "ctx", None),
        P(),
        P(("groups", "tm"), "ctx", None),
        P("tm", "tp"),
        P("tm", "tp"),
        P("tm", "tp"),
        P("tp", "tm"),
        P("tm", "tp"),
        P("tp", "tm"),
        P(None, "tp"),
    )
    return jax.shard_map(
        on_device,
        mesh=mesh,
        in_specs=placed,
        out_specs=P(("groups", "tm"), "ctx", "tp"),
        check_vma=False,
    )
```

```python
import functools

import jax
import jax.numpy as jnp
from jax import lax
from jax.experimental import pallas as pl
from jax.experimental.pallas import tpu as pltpu
from jax.sharding import PartitionSpec as P

HEAD_DIM = 64
KERNEL = 5
MASKED = -1e30
LANES = 128
AXES = ("ctx", "tm", "groups", "tp")


def from_behind(value, axis, steps):
    count = lax.axis_size(axis)
    first, last = (max(0, -steps), min(count, count - steps))
    return lax.ppermute(value, axis, [(source, source + steps) for source in range(first, last)])


def rms_norm(tokens, norm_gain):
    values = tokens.astype(jnp.float32)
    square = jnp.mean(values * values, axis=-1, keepdims=True)
    return (values * lax.rsqrt(square + 1e-05) * norm_gain).astype(jnp.bfloat16)


def across(value, axis, step):
    count = lax.axis_size(axis)
    return lax.ppermute(value, axis, [(source, source ^ step) for source in range(count)])


def two_ways(value, steps):
    pairs = [
        (2 * source + core, 2 * (source ^ steps[core]) + core)
        for source in range(lax.axis_size("ctx"))
        for core in range(2)
    ]
    return lax.ppermute(value, ("ctx", "tp"), pairs)


def convolve(normed_cols, conv_weight):
    frames_here, dancers_here, features_here = normed_cols.shape
    wide = normed_cols.astype(jnp.float32)
    before = from_behind(normed_cols[frames_here - 2 :], "tm", 1).astype(jnp.float32)
    after = from_behind(normed_cols[0:2], "tm", -1).astype(jnp.float32)
    padded = jnp.concatenate([before, wide, after], axis=0)
    convolved = jnp.zeros((frames_here, dancers_here, features_here), jnp.float32)
    for offset in range(KERNEL):
        convolved = convolved + conv_weight[offset] * padded[offset : offset + frames_here]
    return convolved


def begin(sems, pairs):
    copies = [
        pltpu.make_async_copy(source, target, sems.at[n]) for n, (source, target) in enumerate(pairs)
    ]
    for copy in copies:
        copy.start()
    return copies


def end(copies):
    for copy in copies:
        copy.wait()


def slot(index, size):
    return pl.ds(pl.multiple_of(index * size, size), size)


def dot(left, right):
    return jnp.dot(left, right, preferred_element_type=jnp.float32)


def normalise_kernel(n_ctx, mask_in, tokens, gain, full, edge, mask, sems):
    rows, width = tokens.shape
    copies = begin(sems, [(mask_in, mask)])
    values = tokens[...].astype(jnp.float32)
    square = jnp.mean(values * values, axis=-1, keepdims=True)
    full[0:rows, :] = (values * lax.rsqrt(square + 1e-05) * gain[...]).astype(jnp.bfloat16)
    end(copies)
    entries = [
        jnp.full((8, LANES), mask[0, e].astype(jnp.float32), jnp.float32) for e in range(n_ctx)
    ]
    entries.append(jnp.zeros((8, width - n_ctx * LANES), jnp.float32))
    entries = jnp.concatenate(entries, axis=1).astype(jnp.bfloat16)
    full[rows:, :] = entries
    tm, tp = lax.axis_index("tm"), lax.axis_index("tp")
    size, columns = edge.shape
    last = full[rows - size : rows, slot(tp, columns)]
    edge[...] = jnp.where(tm == 0, last, full[0:size, slot(tp, columns)])


def pack_kernel(n_ctx, w_up, w_query, w_key, w_value, packed, sems):
    ctx, groups = lax.axis_index("ctx"), lax.axis_index("groups")
    count = packed.shape[0]
    pairs, column = [], 0
    for w in (w_up, w_query, w_key, w_value):
        size = w.shape[1] // n_ctx
        source = w.at[slot(groups, count), slot(ctx, size)]
        pairs.append((source, packed.at[:, column : column + size]))
        column += size
    end(begin(sems, pairs))


def split_kernel(block, piece):
    size = piece.shape[0]
    upper = lax.axis_index("tp") == 1
    piece[...] = jnp.where(upper, block[block.shape[0] - size :, :], block[0:size, :])


def pack_near_kernel(n_ctx, after, w_up, w_query, w_key, w_value, near, sems):
    ctx = lax.axis_index("ctx")
    pairs, column = [], 0
    for w in (w_up, w_query, w_key, w_value):
        size = w.shape[1] // n_ctx
        pairs.append((w.at[:, slot(ctx, size)], near.at[:, column : column + size]))
        column += size
    end(begin(sems, pairs))


def convolve_kernel(per_frame, tokens, full, halo, taps, base, held):
    tm, tp = lax.axis_index("tm"), lax.axis_index("tp")
    rows, columns = base.shape
    edge = 16
    margin = 2 * per_frame
    near = halo[...].astype(jnp.float32)
    zeros = jnp.zeros((edge, columns), jnp.float32)
    held[0:edge, :] = jnp.where(tm == 1, near, zeros)
    held[edge : edge + rows, :] = full[0:rows, slot(tp, columns)].astype(jnp.float32)
    held[edge + rows :, :] = jnp.where(tm == 0, near, zeros)
    total = tokens[:, slot(tp, columns)].astype(jnp.float32)
    for offset in range(KERNEL):
        start = edge - margin + offset * per_frame
        total += taps[offset : offset + 1, :] * held[start : start + rows, :]
    base[...] = total


def project_kernel(n_ctx, *refs):
    own, block, other_block, piece, other_piece = refs[:5]
    near, far, farther = refs[5:8]
    acts = refs[8 : 8 + n_ctx]
    queries, keys, values, bias, held = refs[8 + n_ctx :]
    ctx, tm, groups, tp = (lax.axis_index(name) for name in AXES)
    rows, depth = own.shape[0] - 8, near.shape[0]
    sources = (
        (own, slot(0, rows), rows),
        (block, slot(1 + tp, rows), rows),
        (other_block, slot(2 - tp, rows), rows),
        (piece, slot(6 + tp, rows // 2), rows // 2),
        (other_piece, slot(7 - tp, rows // 2), rows // 2),
    )
    half = depth // 2
    cuts = ((0, slot(tm, depth), depth), (depth, slot(2 * (1 - tm) + groups, half), half))
    cuts += ((depth + half, slot(2 * (1 - tm) + 1 - groups, half), half),)
    for source, target, size in sources:
        for to, lanes, wide in cuts:
            held[target, to : to + wide] = source[0:size, lanes]
    total = dot(held[:, 0:depth], near[...])
    total += dot(held[:, depth : depth + half], far[...])
    total += dot(held[:, depth + half :], farther[...])
    hidden, wide = acts[0].shape[1], queries.shape[1]
    activated = jax.nn.gelu(total[:, :hidden], approximate=True).astype(jnp.bfloat16)
    for d in range(n_ctx):
        acts[d][...] = activated[d * rows : (d + 1) * rows]
    projected = total[:, hidden:].astype(jnp.bfloat16)
    queries[...] = projected[:, 0:wide]
    keys[...] = projected[:, wide : 2 * wide]
    values[...] = projected[:, 2 * wide :].T
    for j in range(n_ctx):
        lanes = slot(ctx ^ j, LANES)
        one, other = block[rows:, lanes], other_block[rows:, lanes]
        last, other_last = piece[rows // 2 :, lanes], other_piece[rows // 2 :, lanes]
        entries = (
            own[rows:, lanes],
            jnp.where(tp == 0, one, other),
            jnp.where(tp == 0, other, one),
            jnp.where(tp == 0, other_last, last),
        )
        for i, entry in enumerate(entries):
            flag = entry.astype(jnp.float32)
            target = slice(j * LANES, (j + 1) * LANES)
            bias[8 * i : 8 * (i + 1), target] = jnp.where(flag > 0, 0.0, MASKED)


def attend_kernel(n_ctx, i, activated, queries, keys, values, bias, out):
    rows, hidden = activated.shape
    wide = out.shape[1] - hidden
    block = queries[i * rows : (i + 1) * rows, :]
    lane_head = lax.broadcasted_iota(jnp.int32, (1, wide), 1) // HEAD_DIM
    allowed = jnp.concatenate(
        [
            jnp.broadcast_to(bias[8 * i : 8 * i + 1, j * LANES : (j + 1) * LANES], (rows, rows))
            for j in range(n_ctx)
        ],
        axis=0,
    )
    results = []
    for head in range(wide // HEAD_DIM):
        one = jnp.where(lane_head == head, block, jnp.zeros_like(block))
        scores = lax.dot_general(
            keys[...], one, (((1,), (1,)), ((), ())), preferred_element_type=jnp.float32
        )
        scores = scores * 0.125 + allowed
        peak = jnp.max(scores, axis=0, keepdims=True)
        expo = jnp.exp(scores - peak)
        total = jnp.sum(expo, axis=0, keepdims=True)
        mixed = jnp.dot(
            values[head * HEAD_DIM : (head + 1) * HEAD_DIM, :],
            expo.astype(jnp.bfloat16),
            preferred_element_type=jnp.float32,
        )
        results.append(mixed / total)
    out[:, 0:hidden] = activated[...]
    out[:, hidden:] = jnp.concatenate(results, axis=0).T.astype(jnp.bfloat16)


def join_kernel(n_ctx, *refs):
    near_down, near_out, base = refs[:3]
    far_down, farther_down, far_out = refs[3:6]
    parts = refs[6 : 6 + n_ctx]
    keep, send, down, out, acts, atts, sems = refs[6 + n_ctx :]
    ctx, tm, groups, tp = (lax.axis_index(name) for name in AXES)
    hidden, wide = acts.shape[1] // n_ctx, atts.shape[1] // n_ctx
    count = far_down.shape[0]
    pairs = []
    for d in range(n_ctx):
        pairs.append((parts[d].at[:, 0:hidden], acts.at[:, slot(ctx ^ d, hidden)]))
        pairs.append((parts[d].at[:, hidden:], atts.at[:, slot(ctx ^ d, wide)]))
    pairs.append((far_out, out))
    pairs.append((far_down, down.at[slot(groups, count)]))
    pairs.append((farther_down, down.at[slot(1 - groups, count)]))
    copies = begin(sems, pairs)

    end(copies[: 2 * n_ctx])
    near_sum = dot(acts[...], near_down[...]) + dot(atts[...], near_out[...])
    end(copies[2 * n_ctx :])
    far_sum = dot(acts[...], down[...]) + dot(atts[...], out[...])
    same = tm == tp
    keep[...] = jnp.where(same, near_sum, far_sum) + base[...]
    send[...] = jnp.where(same, far_sum, near_sum).astype(jnp.bfloat16)


SMEM = pl.BlockSpec(memory_space=pltpu.SMEM)
VMEM = pl.BlockSpec(memory_space=pltpu.VMEM)
ANY = pl.BlockSpec(memory_space=pl.ANY)


def call(
    kernel, name, outs, ins, scratch=(), flops=0, moved=1 << 20, transcendentals=0, limit=8 << 20
):
    specs, values = zip(*ins)
    return pl.pallas_call(
        kernel,
        out_shape=[jax.ShapeDtypeStruct(shape, dtype) for shape, dtype in outs],
        in_specs=list(specs),
        out_specs=[VMEM] * len(outs),
        scratch_shapes=list(scratch),
        compiler_params=pltpu.CompilerParams(vmem_limit_bytes=limit),
        name=name,
        cost_estimate=pl.CostEstimate(
            flops=flops, bytes_accessed=moved, transcendentals=transcendentals
        ),
    )(*values)


def after(value, *others):
    return lax.optimization_barrier((value, others))[0]


def split_over_ctx(
    tokens, norm_gain, block_mask, w_query, w_key, w_value, w_out, w_up, w_down, conv_weight
):
    n_ctx = lax.axis_size("ctx")
    groups, ctx = lax.axis_index("groups"), lax.axis_index("ctx")
    tm, tp = lax.axis_index("tm"), lax.axis_index("tp")
    frames_here, dancers_here, width = tokens.shape
    rows = frames_here * dancers_here
    depth = w_query.shape[0]
    wide = w_query.shape[1] // n_ctx
    hidden = w_up.shape[1] // n_ctx
    columns = w_out.shape[1]
    packed = hidden + 3 * wide
    bf16, f32 = jnp.bfloat16, jnp.float32
    (packed_a,) = call(
        functools.partial(pack_kernel, n_ctx),
        "pack",
        [((depth // 2, packed), bf16)],
        [(ANY, w) for w in (w_up, w_query, w_key, w_value)],
        [pltpu.SemaphoreType.DMA((4,))],
        limit=(54 << 20) - (700 << 10),
    )
    token_rows = after(tokens, packed_a).reshape(rows, width)
    full, edge = call(
        functools.partial(normalise_kernel, n_ctx),
        "normalise",
        [((rows + 8, width), bf16), ((16, columns), bf16)],
        [
            (ANY, block_mask[0]),
            (VMEM, token_rows),
            (VMEM, norm_gain.reshape(1, width)),
        ],
        [pltpu.SMEM((1, n_ctx), jnp.int32), pltpu.SemaphoreType.DMA((1,))],
    )
    block = two_ways(full, (1, 2))
    (piece,) = call(split_kernel, "split", [((rows // 2 + 8, width), bf16)], [(VMEM, block)])
    piece = two_ways(piece, (2, 1))
    x_a = across(packed_a, "tm", 1)
    y_a = across(x_a, "groups", 1)
    halo = across(edge, "tm", 1)
    other_block = across(block, "tp", 1)
    other_piece = across(piece, "tp", 1)
    half_down = w_down.shape[0] // 2
    sent_down = lax.dynamic_slice_in_dim(w_down, groups * half_down, half_down, 0)
    x_down = across(after(sent_down, packed_a), "tm", 1)
    x_out = across(after(w_out, packed_a), "tm", 1)

    (base,) = call(
        functools.partial(convolve_kernel, dancers_here),
        "convolve",
        [((rows, columns), f32)],
        [
            (VMEM, token_rows),
            (VMEM, full),
            (VMEM, halo),
            (VMEM, conv_weight),
        ],
        [pltpu.VMEM((rows + 32, columns), f32)],
    )
    (near,) = call(
        functools.partial(pack_near_kernel, n_ctx),
        "pack_near",
        [((depth, packed), bf16)],
        [(ANY, w) for w in (base, w_up, w_query, w_key, w_value)],
        [pltpu.SemaphoreType.DMA((4,))],
    )
    *acts, queries, keys, values, bias = call(
        functools.partial(project_kernel, n_ctx),
        "project",
        [((rows, hidden), bf16)] * n_ctx
        + [((n_ctx * rows, wide), bf16)] * 2
        + [((wide, n_ctx * rows), bf16), ((8 * n_ctx, n_ctx * LANES), f32)],
        [(VMEM, value) for value in (full, block, other_block, piece, other_piece)]
        + [(VMEM, value) for value in (near, x_a, y_a)],
        [
            pltpu.VMEM((n_ctx * rows, width), bf16),
        ],
        flops=2 * n_ctx * rows * width * packed,
        moved=4 << 20,
        transcendentals=n_ctx * rows * hidden,
    )
    parts = [None] * n_ctx
    for i in (2, 3, 1, 0):
        (part,) = call(
            functools.partial(attend_kernel, n_ctx, i),
            "attend",
            [((rows, hidden + wide), bf16)],
            [(VMEM, value) for value in (acts[i], queries, keys, values, bias)],
            flops=4 * wide * n_ctx * rows * rows,
            transcendentals=(wide // HEAD_DIM) * n_ctx * rows * rows,
        )
        parts[i] = part
    y_down = across(after(x_down, queries), "groups", 1)
    parts = parts[:1] + [across(parts[i], "ctx", i) for i in range(1, n_ctx)]
    keep, send = call(
        functools.partial(join_kernel, n_ctx),
        "join",
        [((rows, columns), f32), ((rows, columns), bf16)],
        [(VMEM, w_down), (VMEM, w_out), (VMEM, base)]
        + [(ANY, value) for value in (x_down, y_down, x_out)]
        + [(ANY, value) for value in parts],
        [
            pltpu.VMEM(w_down.shape, bf16),
            pltpu.VMEM(w_out.shape, bf16),
            pltpu.VMEM((rows, w_down.shape[0]), bf16),
            pltpu.VMEM((rows, w_out.shape[0]), bf16),
            pltpu.SemaphoreType.DMA((2 * n_ctx + 3,)),
        ],
        flops=4 * rows * columns * n_ctx * (hidden + wide),
        moved=4 << 20,
    )
    other = across(send, "tp", 1).astype(f32)
    return (keep + other).astype(bf16).reshape(frames_here, dancers_here, columns)


def gather_all(
    tokens, norm_gain, block_mask, w_query, w_key, w_value, w_out, w_up, w_down, conv_weight
):
    frames_here, dancers_here, width = tokens.shape
    rows_here = frames_here * dancers_here
    normed_grid = rms_norm(tokens, norm_gain)
    normed = normed_grid.reshape(rows_here, width)
    query_sum, key_sum, value_sum, hidden = tuple(
        jnp.dot(
            normed,
            lax.all_gather(piece, "tm", axis=0, tiled=True),
            preferred_element_type=jnp.float32,
        )
        for piece in (w_query, w_key, w_value, w_up)
    )
    local_heads = query_sum.shape[1] // HEAD_DIM
    queries = query_sum.astype(jnp.bfloat16).reshape(rows_here, local_heads, HEAD_DIM)
    grid = (frames_here, dancers_here, local_heads * HEAD_DIM)
    key_piece = lax.all_gather(
        key_sum.astype(jnp.bfloat16).reshape(grid), "ctx", axis=1, tiled=True
    )
    value_piece = lax.all_gather(
        value_sum.astype(jnp.bfloat16).reshape(grid), "ctx", axis=1, tiled=True
    )
    count = key_piece.shape[1]
    allowed = jnp.tile(jnp.repeat(block_mask[0, 0].astype(jnp.float32), dancers_here), frames_here)
    key_rows = key_piece.reshape(frames_here * count, local_heads, HEAD_DIM)
    value_rows = value_piece.reshape(frames_here * count, local_heads, HEAD_DIM)
    scores = (
        jnp.einsum("qhd,khd->hqk", queries, key_rows, preferred_element_type=jnp.float32) * 0.125
    )
    scores = jnp.where(allowed[None, None, :] > 0, scores, MASKED)
    expo = jnp.exp(scores - jnp.max(scores, axis=-1, keepdims=True)) * allowed[None, None, :]
    total = jnp.sum(expo, axis=-1)
    mixed = jnp.einsum(
        "hqk,khd->hqd", expo.astype(jnp.bfloat16), value_rows, preferred_element_type=jnp.float32
    )
    attended = (
        (mixed / total[:, :, None])
        .transpose(1, 0, 2)
        .reshape(rows_here, local_heads * HEAD_DIM)
        .astype(jnp.bfloat16)
    )
    activated = jax.nn.gelu(hidden, approximate=True).astype(jnp.bfloat16)
    out_full = lax.all_gather(w_out, "tm", axis=1, tiled=True)
    down_full = lax.all_gather(w_down, "tm", axis=1, tiled=True)
    branches = jnp.dot(attended, out_full, preferred_element_type=jnp.float32)
    branches = branches + jnp.dot(activated, down_full, preferred_element_type=jnp.float32)
    mine = lax.psum_scatter(
        branches.astype(jnp.bfloat16), "tp", scatter_dimension=1, tiled=True
    ).astype(jnp.float32)
    features_here = mine.shape[1]
    first_feature = lax.axis_index("tp") * features_here
    normed_cols = lax.dynamic_slice_in_dim(normed_grid, first_feature, features_here, 2)
    token_cols = lax.dynamic_slice_in_dim(tokens, first_feature, features_here, 2)
    result = (
        token_cols.astype(jnp.float32)
        + mine.reshape(frames_here, dancers_here, features_here)
        + convolve(normed_cols, conv_weight)
    )
    return result.astype(jnp.bfloat16)


def solution(mesh):
    n_ctx, n_tm = mesh.shape["ctx"], mesh.shape["tm"]

    def on_device(*arrays):
        local_heads = arrays[3].shape[1] // HEAD_DIM
        pairs = n_tm == 2 and mesh.shape["groups"] == 2 and mesh.shape["tp"] == 2
        even = n_ctx == 4 and local_heads == 2 * n_ctx
        chosen = split_over_ctx if pairs and even else gather_all
        return chosen(*arrays)

    placed = (
        P(("groups", "tm"), "ctx", None),
        P(),
        P(("groups", "tm"), "ctx", None),
        P("tm", "tp"),
        P("tm", "tp"),
        P("tm", "tp"),
        P("tp", "tm"),
        P("tm", "tp"),
        P("tp", "tm"),
        P(None, "tp"),
    )
    return jax.shard_map(
        on_device,
        mesh=mesh,
        in_specs=placed,
        out_specs=P(("groups", "tm"), "ctx", "tp"),
        check_vma=False,
    )
```

```python
import functools

import jax
import jax.numpy as jnp
from jax import lax
from jax.experimental import pallas as pl
from jax.experimental.pallas import tpu as pltpu
from jax.sharding import PartitionSpec as P

HEAD_DIM = 64
KERNEL = 5
MASKED = -1e30
LANES = 128
AXES = ("ctx", "tm", "groups", "tp")


def from_behind(value, axis, steps):
    count = lax.axis_size(axis)
    first, last = (max(0, -steps), min(count, count - steps))
    return lax.ppermute(value, axis, [(source, source + steps) for source in range(first, last)])


def rms_norm(tokens, norm_gain):
    values = tokens.astype(jnp.float32)
    square = jnp.mean(values * values, axis=-1, keepdims=True)
    return (values * lax.rsqrt(square + 1e-05) * norm_gain).astype(jnp.bfloat16)


def across(value, axis, step):
    count = lax.axis_size(axis)
    return lax.ppermute(value, axis, [(source, source ^ step) for source in range(count)])


def two_ways(value, steps):
    pairs = [
        (2 * source + core, 2 * (source ^ steps[core]) + core)
        for source in range(lax.axis_size("ctx"))
        for core in range(2)
    ]
    return lax.ppermute(value, ("ctx", "tp"), pairs)


def convolve(normed_cols, conv_weight):
    frames_here, dancers_here, features_here = normed_cols.shape
    wide = normed_cols.astype(jnp.float32)
    before = from_behind(normed_cols[frames_here - 2 :], "tm", 1).astype(jnp.float32)
    after = from_behind(normed_cols[0:2], "tm", -1).astype(jnp.float32)
    padded = jnp.concatenate([before, wide, after], axis=0)
    convolved = jnp.zeros((frames_here, dancers_here, features_here), jnp.float32)
    for offset in range(KERNEL):
        convolved = convolved + conv_weight[offset] * padded[offset : offset + frames_here]
    return convolved


def begin(sems, pairs):
    copies = [
        pltpu.make_async_copy(source, target, sems.at[n]) for n, (source, target) in enumerate(pairs)
    ]
    for copy in copies:
        copy.start()
    return copies


def end(copies):
    for copy in copies:
        copy.wait()


def slot(index, size):
    return pl.ds(pl.multiple_of(index * size, size), size)


def dot(left, right):
    return jnp.dot(left, right, preferred_element_type=jnp.float32)


def normalise_kernel(n_ctx, mask_in, tokens, gain, full, edge, mask, sems):
    rows, width = tokens.shape
    copies = begin(sems, [(mask_in, mask)])
    values = tokens[...].astype(jnp.float32)
    square = jnp.mean(values * values, axis=-1, keepdims=True)
    full[0:rows, :] = (values * lax.rsqrt(square + 1e-05) * gain[...]).astype(jnp.bfloat16)
    end(copies)
    entries = [
        jnp.full((8, LANES), mask[0, e].astype(jnp.float32), jnp.float32) for e in range(n_ctx)
    ]
    entries.append(jnp.zeros((8, width - n_ctx * LANES), jnp.float32))
    entries = jnp.concatenate(entries, axis=1).astype(jnp.bfloat16)
    full[rows:, :] = entries
    tm, tp = lax.axis_index("tm"), lax.axis_index("tp")
    size, columns = edge.shape
    last = full[rows - size : rows, slot(tp, columns)]
    edge[...] = jnp.where(tm == 0, last, full[0:size, slot(tp, columns)])


def pack_kernel(n_ctx, w_up, w_query, w_key, w_value, packed, sems):
    ctx, groups = lax.axis_index("ctx"), lax.axis_index("groups")
    count = packed.shape[0]
    pairs, column = [], 0
    for w in (w_up, w_query, w_key, w_value):
        size = w.shape[1] // n_ctx
        source = w.at[slot(groups, count), slot(ctx, size)]
        pairs.append((source, packed.at[:, column : column + size]))
        column += size
    end(begin(sems, pairs))


def split_kernel(block, piece):
    size = piece.shape[0]
    upper = lax.axis_index("tp") == 1
    piece[...] = jnp.where(upper, block[block.shape[0] - size :, :], block[0:size, :])


def pack_near_kernel(n_ctx, after, w_up, w_query, w_key, w_value, near, sems):
    ctx = lax.axis_index("ctx")
    pairs, column = [], 0
    for w in (w_up, w_query, w_key, w_value):
        size = w.shape[1] // n_ctx
        pairs.append((w.at[:, slot(ctx, size)], near.at[:, column : column + size]))
        column += size
    end(begin(sems, pairs))


def convolve_kernel(per_frame, tokens, full, received, taps, base, held):
    tm, tp = lax.axis_index("tm"), lax.axis_index("tp")
    rows, columns = base.shape
    edge = 16
    margin = 2 * per_frame
    near = received[received.shape[0] - edge :, :].astype(jnp.float32)
    zeros = jnp.zeros((edge, columns), jnp.float32)
    held[0:edge, :] = jnp.where(tm == 1, near, zeros)
    held[edge : edge + rows, :] = full[0:rows, slot(tp, columns)].astype(jnp.float32)
    held[edge + rows :, :] = jnp.where(tm == 0, near, zeros)
    total = tokens[:, slot(tp, columns)].astype(jnp.float32)
    for offset in range(KERNEL):
        start = edge - margin + offset * per_frame
        total += taps[offset : offset + 1, :] * held[start : start + rows, :]
    base[...] = total


def project_kernel(n_ctx, *refs):
    own, block, other_block, piece, other_piece = refs[:5]
    near, far, farther = refs[5:8]
    acts = refs[8 : 8 + n_ctx]
    queries, keys, values, bias, held = refs[8 + n_ctx :]
    ctx, tm, groups, tp = (lax.axis_index(name) for name in AXES)
    rows, depth = own.shape[0] - 8, near.shape[0]
    sources = (
        (own, slot(0, rows), rows),
        (block, slot(1 + tp, rows), rows),
        (other_block, slot(2 - tp, rows), rows),
        (piece, slot(6 + tp, rows // 2), rows // 2),
        (other_piece, slot(7 - tp, rows // 2), rows // 2),
    )
    half = depth // 2
    cuts = ((0, slot(tm, depth), depth), (depth, slot(2 * (1 - tm) + groups, half), half))
    cuts += ((depth + half, slot(2 * (1 - tm) + 1 - groups, half), half),)
    for source, target, size in sources:
        for to, lanes, wide in cuts:
            held[target, to : to + wide] = source[0:size, lanes]
    total = dot(held[:, 0:depth], near[...])
    total += dot(held[:, depth : depth + half], far[...])
    total += dot(held[:, depth + half :], farther[...])
    hidden, wide = acts[0].shape[1], queries.shape[1]
    activated = jax.nn.gelu(total[:, :hidden], approximate=True).astype(jnp.bfloat16)
    for d in range(n_ctx):
        acts[d][...] = activated[d * rows : (d + 1) * rows]
    projected = total[:, hidden:].astype(jnp.bfloat16)
    queries[...] = projected[:, 0:wide]
    keys[...] = projected[:, wide : 2 * wide]
    values[...] = projected[:, 2 * wide :].T
    for j in range(n_ctx):
        lanes = slot(ctx ^ j, LANES)
        one, other = block[rows:, lanes], other_block[rows:, lanes]
        last, other_last = piece[rows // 2 :, lanes], other_piece[rows // 2 :, lanes]
        entries = (
            own[rows:, lanes],
            jnp.where(tp == 0, one, other),
            jnp.where(tp == 0, other, one),
            jnp.where(tp == 0, other_last, last),
        )
        for i, entry in enumerate(entries):
            flag = entry.astype(jnp.float32)
            target = slice(j * LANES, (j + 1) * LANES)
            bias[8 * i : 8 * (i + 1), target] = jnp.where(flag > 0, 0.0, MASKED)


def attend_kernel(n_ctx, i, activated, queries, keys, values, bias, out):
    rows, hidden = activated.shape
    wide = out.shape[1] - hidden
    block = queries[i * rows : (i + 1) * rows, :]
    lane_head = lax.broadcasted_iota(jnp.int32, (1, wide), 1) // HEAD_DIM
    allowed = jnp.concatenate(
        [
            jnp.broadcast_to(bias[8 * i : 8 * i + 1, j * LANES : (j + 1) * LANES], (rows, rows))
            for j in range(n_ctx)
        ],
        axis=0,
    )
    results = []
    for head in range(wide // HEAD_DIM):
        one = jnp.where(lane_head == head, block, jnp.zeros_like(block))
        scores = lax.dot_general(
            keys[...], one, (((1,), (1,)), ((), ())), preferred_element_type=jnp.float32
        )
        scores = scores * 0.125 + allowed
        peak = jnp.max(scores, axis=0, keepdims=True)
        expo = jnp.exp(scores - peak)
        total = jnp.sum(expo, axis=0, keepdims=True)
        mixed = jnp.dot(
            values[head * HEAD_DIM : (head + 1) * HEAD_DIM, :],
            expo.astype(jnp.bfloat16),
            preferred_element_type=jnp.float32,
        )
        results.append(mixed / total)
    out[:, 0:hidden] = activated[...]
    out[:, hidden:] = jnp.concatenate(results, axis=0).T.astype(jnp.bfloat16)


def join_kernel(n_ctx, *refs):
    near_down, near_out, base = refs[:3]
    far_down, farther_down, far_out = refs[3:6]
    parts = refs[6 : 6 + n_ctx]
    keep, send, down, out, acts, atts, sems = refs[6 + n_ctx :]
    ctx, tm, groups, tp = (lax.axis_index(name) for name in AXES)
    hidden, wide = acts.shape[1] // n_ctx, atts.shape[1] // n_ctx
    count = near_down.shape[0] // 2
    pairs = []
    for d in range(n_ctx):
        pairs.append((parts[d].at[:, 0:hidden], acts.at[:, slot(ctx ^ d, hidden)]))
        pairs.append((parts[d].at[:, hidden:], atts.at[:, slot(ctx ^ d, wide)]))
    pairs.append((far_out, out))
    pairs.append((far_down.at[0:count], down.at[slot(groups, count)]))
    pairs.append((farther_down.at[0:count], down.at[slot(1 - groups, count)]))
    copies = begin(sems, pairs)

    end(copies[: 2 * n_ctx])
    near_sum = dot(acts[...], near_down[...]) + dot(atts[...], near_out[...])
    end(copies[2 * n_ctx :])
    far_sum = dot(acts[...], down[...]) + dot(atts[...], out[...])
    same = tm == tp
    keep[...] = jnp.where(same, near_sum, far_sum) + base[...]
    send[...] = jnp.where(same, far_sum, near_sum).astype(jnp.bfloat16)


SMEM = pl.BlockSpec(memory_space=pltpu.SMEM)
VMEM = pl.BlockSpec(memory_space=pltpu.VMEM)
ANY = pl.BlockSpec(memory_space=pl.ANY)


def call(
    kernel, name, outs, ins, scratch=(), flops=0, moved=1 << 20, transcendentals=0, limit=8 << 20
):
    specs, values = zip(*ins)
    return pl.pallas_call(
        kernel,
        out_shape=[jax.ShapeDtypeStruct(shape, dtype) for shape, dtype in outs],
        in_specs=list(specs),
        out_specs=[VMEM] * len(outs),
        scratch_shapes=list(scratch),
        compiler_params=pltpu.CompilerParams(vmem_limit_bytes=limit),
        name=name,
        cost_estimate=pl.CostEstimate(
            flops=flops, bytes_accessed=moved, transcendentals=transcendentals
        ),
    )(*values)


def after(value, *others):
    return lax.optimization_barrier((value, others))[0]


def split_over_ctx(
    tokens, norm_gain, block_mask, w_query, w_key, w_value, w_out, w_up, w_down, conv_weight
):
    n_ctx = lax.axis_size("ctx")
    groups, ctx = lax.axis_index("groups"), lax.axis_index("ctx")
    tm, tp = lax.axis_index("tm"), lax.axis_index("tp")
    frames_here, dancers_here, width = tokens.shape
    rows = frames_here * dancers_here
    depth = w_query.shape[0]
    wide = w_query.shape[1] // n_ctx
    hidden = w_up.shape[1] // n_ctx
    columns = w_out.shape[1]
    packed = hidden + 3 * wide
    bf16, f32 = jnp.bfloat16, jnp.float32
    (packed_a,) = call(
        functools.partial(pack_kernel, n_ctx),
        "pack",
        [((depth // 2, packed), bf16)],
        [(ANY, w) for w in (w_up, w_query, w_key, w_value)],
        [pltpu.SemaphoreType.DMA((4,))],
        limit=(54 << 20) - (700 << 10),
    )
    token_rows = after(tokens, packed_a).reshape(rows, width)
    full, edge = call(
        functools.partial(normalise_kernel, n_ctx),
        "normalise",
        [((rows + 8, width), bf16), ((16, columns), bf16)],
        [
            (ANY, block_mask[0]),
            (VMEM, token_rows),
            (VMEM, norm_gain.reshape(1, width)),
        ],
        [pltpu.SMEM((1, n_ctx), jnp.int32), pltpu.SemaphoreType.DMA((1,))],
    )
    x_a = across(packed_a, "tm", 1)
    y_a = across(x_a, "groups", 1)
    half_down = w_down.shape[0] // 2
    sent_down = lax.dynamic_slice_in_dim(w_down, groups * half_down, half_down, 0)
    sent_down = jnp.concatenate([sent_down, edge], axis=0)
    x_down = across(after(sent_down, packed_a), "tm", 1)
    x_out = across(after(w_out, packed_a), "tm", 1)

    (near,) = call(
        functools.partial(pack_near_kernel, n_ctx),
        "pack_near",
        [((depth, packed), bf16)],
        [(ANY, w) for w in (packed_a, w_up, w_query, w_key, w_value)],
        [pltpu.SemaphoreType.DMA((4,))],
    )
    block = two_ways(full, (1, 2))
    other_block = across(block, "tp", 1)
    (piece,) = call(split_kernel, "split", [((rows // 2 + 8, width), bf16)], [(VMEM, block)])
    piece = two_ways(piece, (2, 1))
    other_piece = across(piece, "tp", 1)
    *acts, queries, keys, values, bias = call(
        functools.partial(project_kernel, n_ctx),
        "project",
        [((rows, hidden), bf16)] * n_ctx
        + [((n_ctx * rows, wide), bf16)] * 2
        + [((wide, n_ctx * rows), bf16), ((8 * n_ctx, n_ctx * LANES), f32)],
        [(VMEM, value) for value in (full, block, other_block, piece, other_piece)]
        + [(VMEM, value) for value in (near, x_a, y_a)],
        [
            pltpu.VMEM((n_ctx * rows, width), bf16),
        ],
        flops=2 * n_ctx * rows * width * packed,
        moved=4 << 20,
        transcendentals=n_ctx * rows * hidden,
    )
    parts = [None] * n_ctx
    for i in (2, 3, 1, 0):
        (part,) = call(
            functools.partial(attend_kernel, n_ctx, i),
            "attend",
            [((rows, hidden + wide), bf16)],
            [(VMEM, value) for value in (acts[i], queries, keys, values, bias)],
            flops=4 * wide * n_ctx * rows * rows,
            transcendentals=(wide // HEAD_DIM) * n_ctx * rows * rows,
        )
        parts[i] = part
    y_down = across(after(x_down, queries), "groups", 1)
    parts = parts[:1] + [across(parts[i], "ctx", i) for i in range(1, n_ctx)]
    (base,) = call(
        functools.partial(convolve_kernel, dancers_here),
        "convolve",
        [((rows, columns), f32)],
        [
            (VMEM, token_rows),
            (VMEM, full),
            (VMEM, x_down),
            (VMEM, conv_weight),
        ],
        [pltpu.VMEM((rows + 32, columns), f32)],
    )
    keep, send = call(
        functools.partial(join_kernel, n_ctx),
        "join",
        [((rows, columns), f32), ((rows, columns), bf16)],
        [(VMEM, w_down), (VMEM, w_out), (VMEM, base)]
        + [(ANY, value) for value in (x_down, y_down, x_out)]
        + [(ANY, value) for value in parts],
        [
            pltpu.VMEM(w_down.shape, bf16),
            pltpu.VMEM(w_out.shape, bf16),
            pltpu.VMEM((rows, w_down.shape[0]), bf16),
            pltpu.VMEM((rows, w_out.shape[0]), bf16),
            pltpu.SemaphoreType.DMA((2 * n_ctx + 3,)),
        ],
        flops=4 * rows * columns * n_ctx * (hidden + wide),
        moved=4 << 20,
    )
    other = across(send, "tp", 1).astype(f32)
    return (keep + other).astype(bf16).reshape(frames_here, dancers_here, columns)


def gather_all(
    tokens, norm_gain, block_mask, w_query, w_key, w_value, w_out, w_up, w_down, conv_weight
):
    frames_here, dancers_here, width = tokens.shape
    rows_here = frames_here * dancers_here
    normed_grid = rms_norm(tokens, norm_gain)
    normed = normed_grid.reshape(rows_here, width)
    query_sum, key_sum, value_sum, hidden = tuple(
        jnp.dot(
            normed,
            lax.all_gather(piece, "tm", axis=0, tiled=True),
            preferred_element_type=jnp.float32,
        )
        for piece in (w_query, w_key, w_value, w_up)
    )
    local_heads = query_sum.shape[1] // HEAD_DIM
    queries = query_sum.astype(jnp.bfloat16).reshape(rows_here, local_heads, HEAD_DIM)
    grid = (frames_here, dancers_here, local_heads * HEAD_DIM)
    key_piece = lax.all_gather(
        key_sum.astype(jnp.bfloat16).reshape(grid), "ctx", axis=1, tiled=True
    )
    value_piece = lax.all_gather(
        value_sum.astype(jnp.bfloat16).reshape(grid), "ctx", axis=1, tiled=True
    )
    count = key_piece.shape[1]
    allowed = jnp.tile(jnp.repeat(block_mask[0, 0].astype(jnp.float32), dancers_here), frames_here)
    key_rows = key_piece.reshape(frames_here * count, local_heads, HEAD_DIM)
    value_rows = value_piece.reshape(frames_here * count, local_heads, HEAD_DIM)
    scores = (
        jnp.einsum("qhd,khd->hqk", queries, key_rows, preferred_element_type=jnp.float32) * 0.125
    )
    scores = jnp.where(allowed[None, None, :] > 0, scores, MASKED)
    expo = jnp.exp(scores - jnp.max(scores, axis=-1, keepdims=True)) * allowed[None, None, :]
    total = jnp.sum(expo, axis=-1)
    mixed = jnp.einsum(
        "hqk,khd->hqd", expo.astype(jnp.bfloat16), value_rows, preferred_element_type=jnp.float32
    )
    attended = (
        (mixed / total[:, :, None])
        .transpose(1, 0, 2)
        .reshape(rows_here, local_heads * HEAD_DIM)
        .astype(jnp.bfloat16)
    )
    activated = jax.nn.gelu(hidden, approximate=True).astype(jnp.bfloat16)
    out_full = lax.all_gather(w_out, "tm", axis=1, tiled=True)
    down_full = lax.all_gather(w_down, "tm", axis=1, tiled=True)
    branches = jnp.dot(attended, out_full, preferred_element_type=jnp.float32)
    branches = branches + jnp.dot(activated, down_full, preferred_element_type=jnp.float32)
    mine = lax.psum_scatter(
        branches.astype(jnp.bfloat16), "tp", scatter_dimension=1, tiled=True
    ).astype(jnp.float32)
    features_here = mine.shape[1]
    first_feature = lax.axis_index("tp") * features_here
    normed_cols = lax.dynamic_slice_in_dim(normed_grid, first_feature, features_here, 2)
    token_cols = lax.dynamic_slice_in_dim(tokens, first_feature, features_here, 2)
    result = (
        token_cols.astype(jnp.float32)
        + mine.reshape(frames_here, dancers_here, features_here)
        + convolve(normed_cols, conv_weight)
    )
    return result.astype(jnp.bfloat16)


def solution(mesh):
    n_ctx, n_tm = mesh.shape["ctx"], mesh.shape["tm"]

    def on_device(*arrays):
        local_heads = arrays[3].shape[1] // HEAD_DIM
        pairs = n_tm == 2 and mesh.shape["groups"] == 2 and mesh.shape["tp"] == 2
        even = n_ctx == 4 and local_heads == 2 * n_ctx
        chosen = split_over_ctx if pairs and even else gather_all
        return chosen(*arrays)

    placed = (
        P(("groups", "tm"), "ctx", None),
        P(),
        P(("groups", "tm"), "ctx", None),
        P("tm", "tp"),
        P("tm", "tp"),
        P("tm", "tp"),
        P("tp", "tm"),
        P("tm", "tp"),
        P("tp", "tm"),
        P(None, "tp"),
    )
    return jax.shard_map(
        on_device,
        mesh=mesh,
        in_specs=placed,
        out_specs=P(("groups", "tm"), "ctx", "tp"),
        check_vma=False,
    )
```

```python
import functools

import jax
import jax.numpy as jnp
from jax import lax
from jax.experimental import pallas as pl
from jax.experimental.pallas import tpu as pltpu
from jax.sharding import PartitionSpec as P

HEAD_DIM = 64
KERNEL = 5
MASKED = -1e30
LANES = 128
AXES = ("ctx", "tm", "groups", "tp")


def from_behind(value, axis, steps):
    count = lax.axis_size(axis)
    first, last = (max(0, -steps), min(count, count - steps))
    return lax.ppermute(value, axis, [(source, source + steps) for source in range(first, last)])


def rms_norm(tokens, norm_gain):
    values = tokens.astype(jnp.float32)
    square = jnp.mean(values * values, axis=-1, keepdims=True)
    return (values * lax.rsqrt(square + 1e-05) * norm_gain).astype(jnp.bfloat16)


def across(value, axis, step):
    count = lax.axis_size(axis)
    return lax.ppermute(value, axis, [(source, source ^ step) for source in range(count)])


def two_ways(value, steps):
    pairs = [
        (2 * source + core, 2 * (source ^ steps[core]) + core)
        for source in range(lax.axis_size("ctx"))
        for core in range(2)
    ]
    return lax.ppermute(value, ("ctx", "tp"), pairs)


def convolve(normed_cols, conv_weight):
    frames_here, dancers_here, features_here = normed_cols.shape
    wide = normed_cols.astype(jnp.float32)
    before = from_behind(normed_cols[frames_here - 2 :], "tm", 1).astype(jnp.float32)
    after = from_behind(normed_cols[0:2], "tm", -1).astype(jnp.float32)
    padded = jnp.concatenate([before, wide, after], axis=0)
    convolved = jnp.zeros((frames_here, dancers_here, features_here), jnp.float32)
    for offset in range(KERNEL):
        convolved = convolved + conv_weight[offset] * padded[offset : offset + frames_here]
    return convolved


def begin(sems, pairs):
    copies = [
        pltpu.make_async_copy(source, target, sems.at[n]) for n, (source, target) in enumerate(pairs)
    ]
    for copy in copies:
        copy.start()
    return copies


def end(copies):
    for copy in copies:
        copy.wait()


def slot(index, size):
    return pl.ds(pl.multiple_of(index * size, size), size)


def dot(left, right):
    return jnp.dot(left, right, preferred_element_type=jnp.float32)


def normalise_kernel(n_ctx, mask_in, tokens, gain, full, own, mine, edge, mask, sems):
    rows, width = tokens.shape
    copies = begin(sems, [(mask_in, mask)])
    values = tokens[...].astype(jnp.float32)
    square = jnp.mean(values * values, axis=-1, keepdims=True)
    full[0:rows, :] = (values * lax.rsqrt(square + 1e-05) * gain[...]).astype(jnp.bfloat16)
    end(copies)
    entries = [
        jnp.full((8, LANES), mask[0, e].astype(jnp.float32), jnp.float32) for e in range(n_ctx)
    ]
    entries.append(jnp.zeros((8, width - n_ctx * LANES), jnp.float32))
    entries = jnp.concatenate(entries, axis=1).astype(jnp.bfloat16)
    full[rows:, :] = entries
    tm, tp = lax.axis_index("tm"), lax.axis_index("tp")
    own[...] = full[...]
    size, columns = edge.shape
    mine[...] = full[0:rows, slot(tp, columns)]
    edge[...] = jnp.where(tm == 0, mine[rows - size :, :], mine[0:size, :])


def pack_kernel(n_ctx, w_up, w_query, w_key, w_value, packed, sems):
    ctx, groups = lax.axis_index("ctx"), lax.axis_index("groups")
    count = packed.shape[0]
    pairs, column = [], 0
    for w in (w_up, w_query, w_key, w_value):
        size = w.shape[1] // n_ctx
        source = w.at[slot(groups, count), slot(ctx, size)]
        pairs.append((source, packed.at[:, column : column + size]))
        column += size
    end(begin(sems, pairs))


def split_kernel(block, piece):
    size = piece.shape[0]
    upper = lax.axis_index("tp") == 1
    piece[...] = jnp.where(upper, block[block.shape[0] - size :, :], block[0:size, :])


def pack_near_kernel(n_ctx, after, w_up, w_query, w_key, w_value, near, sems):
    ctx = lax.axis_index("ctx")
    pairs, column = [], 0
    for w in (w_up, w_query, w_key, w_value):
        size = w.shape[1] // n_ctx
        pairs.append((w.at[:, slot(ctx, size)], near.at[:, column : column + size]))
        column += size
    end(begin(sems, pairs))


def convolve_kernel(per_frame, tokens, mine, received, taps, last0, last1, base, held):
    tm, tp = lax.axis_index("tm"), lax.axis_index("tp")
    rows, columns = base.shape
    edge = 16
    margin = 2 * per_frame
    near = received[received.shape[0] - edge :, :].astype(jnp.float32)
    zeros = jnp.zeros((edge, columns), jnp.float32)
    held[0:edge, :] = jnp.where(tm == 1, near, zeros)
    held[edge : edge + rows, :] = mine[...].astype(jnp.float32)
    held[edge + rows :, :] = jnp.where(tm == 0, near, zeros)
    total = tokens[:, slot(tp, columns)].astype(jnp.float32)
    for offset in range(KERNEL):
        start = edge - margin + offset * per_frame
        total += taps[offset : offset + 1, :] * held[start : start + rows, :]
    base[...] = total


def project_kernel(n_ctx, *refs):
    own, block, other_block, piece, other_piece = refs[:5]
    near, far, farther = refs[5:8]
    acts = refs[8 : 8 + n_ctx]
    queries, keys, values, bias, held = refs[8 + n_ctx :]
    ctx, tm, groups, tp = (lax.axis_index(name) for name in AXES)
    rows, depth = own.shape[0] - 8, near.shape[0]
    sources = (
        (own, slot(0, rows), rows),
        (block, slot(1 + tp, rows), rows),
        (other_block, slot(2 - tp, rows), rows),
        (piece, slot(6 + tp, rows // 2), rows // 2),
        (other_piece, slot(7 - tp, rows // 2), rows // 2),
    )
    half = depth // 2
    cuts = ((0, slot(tm, depth), depth), (depth, slot(2 * (1 - tm) + groups, half), half))
    cuts += ((depth + half, slot(2 * (1 - tm) + 1 - groups, half), half),)
    for source, target, size in sources:
        for to, lanes, wide in cuts:
            held[target, to : to + wide] = source[0:size, lanes]
    total = dot(held[:, 0:depth], near[...])
    total += dot(held[:, depth : depth + half], far[...])
    total += dot(held[:, depth + half :], farther[...])
    hidden, wide = acts[0].shape[1], queries.shape[1]
    activated = jax.nn.gelu(total[:, :hidden], approximate=True).astype(jnp.bfloat16)
    for d in range(n_ctx):
        acts[d][...] = activated[d * rows : (d + 1) * rows]
    projected = total[:, hidden:].astype(jnp.bfloat16)
    queries[...] = projected[:, 0:wide]
    keys[...] = projected[:, wide : 2 * wide]
    values[...] = projected[:, 2 * wide :].T
    for j in range(n_ctx):
        lanes = slot(ctx ^ j, LANES)
        one, other = block[rows:, lanes], other_block[rows:, lanes]
        last, other_last = piece[rows // 2 :, lanes], other_piece[rows // 2 :, lanes]
        entries = (
            own[rows:, lanes],
            jnp.where(tp == 0, one, other),
            jnp.where(tp == 0, other, one),
            jnp.where(tp == 0, other_last, last),
        )
        for i, entry in enumerate(entries):
            flag = entry.astype(jnp.float32)
            target = slice(j * LANES, (j + 1) * LANES)
            bias[8 * i : 8 * (i + 1), target] = jnp.where(flag > 0, 0.0, MASKED)


def attend_kernel(n_ctx, blocks, *refs):
    count = len(blocks)
    acts, (queries, keys, values, bias) = refs[:count], refs[count : count + 4]
    outs = refs[count + 4 :]
    rows, hidden = acts[0].shape
    wide = outs[0].shape[1] - hidden
    lane_head = lax.broadcasted_iota(jnp.int32, (1, wide), 1) // HEAD_DIM
    for n, i in enumerate(blocks):
        block = queries[i * rows : (i + 1) * rows, :]
        allowed = jnp.concatenate(
            [
                jnp.broadcast_to(
                    bias[8 * i : 8 * i + 1, j * LANES : (j + 1) * LANES], (rows, rows)
                )
                for j in range(n_ctx)
            ],
            axis=0,
        )
        results = []
        for head in range(wide // HEAD_DIM):
            one = jnp.where(lane_head == head, block, jnp.zeros_like(block))
            scores = lax.dot_general(
                keys[...], one, (((1,), (1,)), ((), ())), preferred_element_type=jnp.float32
            )
            scores = scores * 0.125 + allowed
            peak = jnp.max(scores, axis=0, keepdims=True)
            expo = jnp.exp(scores - peak)
            total = jnp.sum(expo, axis=0, keepdims=True)
            mixed = dot(
                values[head * HEAD_DIM : (head + 1) * HEAD_DIM, :], expo.astype(jnp.bfloat16)
            )
            results.append(mixed / total)
        outs[n][:, 0:hidden] = acts[n][...]
        outs[n][:, hidden:] = jnp.concatenate(results, axis=0).T.astype(jnp.bfloat16)


def join_kernel(n_ctx, *refs):
    near_down, near_out, base = refs[:3]
    far_down, farther_down, far_out = refs[3:6]
    parts = refs[6 : 6 + n_ctx]
    keep, send, down, out, acts, atts, sems = refs[6 + n_ctx :]
    ctx, tm, groups, tp = (lax.axis_index(name) for name in AXES)
    hidden, wide = acts.shape[1] // n_ctx, atts.shape[1] // n_ctx
    count = farther_down.shape[0] - 16
    pairs = []
    for d in range(n_ctx):
        pairs.append((parts[d].at[:, 0:hidden], acts.at[:, slot(ctx ^ d, hidden)]))
        pairs.append((parts[d].at[:, hidden:], atts.at[:, slot(ctx ^ d, wide)]))
    pairs.append((far_out.at[0 : out.shape[0]], out))
    pairs.append((far_out.at[out.shape[0] :], down.at[2 * count :]))
    pairs.append((far_down.at[0:count], down.at[slot(groups, count)]))
    pairs.append((farther_down.at[0:count], down.at[slot(1 - groups, count)]))
    copies = begin(sems, pairs)

    end(copies[: 2 * n_ctx])
    near_sum = dot(acts[...], near_down[...]) + dot(atts[...], near_out[...])
    end(copies[2 * n_ctx :])
    far_sum = dot(acts[...], down[...]) + dot(atts[...], out[...])
    same = tm == tp
    keep[...] = jnp.where(same, near_sum, far_sum) + base[...]
    send[...] = jnp.where(same, far_sum, near_sum).astype(jnp.bfloat16)


SMEM = pl.BlockSpec(memory_space=pltpu.SMEM)
VMEM = pl.BlockSpec(memory_space=pltpu.VMEM)
ANY = pl.BlockSpec(memory_space=pl.ANY)


def call(
    kernel, name, outs, ins, scratch=(), flops=0, moved=1 << 20, transcendentals=0, limit=8 << 20
):
    specs, values = zip(*ins)
    return pl.pallas_call(
        kernel,
        out_shape=[jax.ShapeDtypeStruct(shape, dtype) for shape, dtype in outs],
        in_specs=list(specs),
        out_specs=[VMEM] * len(outs),
        scratch_shapes=list(scratch),
        compiler_params=pltpu.CompilerParams(vmem_limit_bytes=limit),
        name=name,
        cost_estimate=pl.CostEstimate(
            flops=flops, bytes_accessed=moved, transcendentals=transcendentals
        ),
    )(*values)


def after(value, *others):
    return lax.optimization_barrier((value, others))[0]


def split_over_ctx(
    tokens, norm_gain, block_mask, w_query, w_key, w_value, w_out, w_up, w_down, conv_weight
):
    n_ctx = lax.axis_size("ctx")
    groups, ctx = lax.axis_index("groups"), lax.axis_index("ctx")
    tm, tp = lax.axis_index("tm"), lax.axis_index("tp")
    frames_here, dancers_here, width = tokens.shape
    rows = frames_here * dancers_here
    depth = w_query.shape[0]
    wide = w_query.shape[1] // n_ctx
    hidden = w_up.shape[1] // n_ctx
    columns = w_out.shape[1]
    packed = hidden + 3 * wide
    bf16, f32 = jnp.bfloat16, jnp.float32
    (packed_a,) = call(
        functools.partial(pack_kernel, n_ctx),
        "pack",
        [((depth // 2, packed), bf16)],
        [(ANY, w) for w in (w_up, w_query, w_key, w_value)],
        [pltpu.SemaphoreType.DMA((4,))],
        limit=(54 << 20) - (700 << 10),
    )
    token_rows = after(tokens, packed_a).reshape(rows, width)
    full, own, mine, edge = call(
        functools.partial(normalise_kernel, n_ctx),
        "normalise",
        [((rows + 8, width), bf16)] * 2 + [((rows, columns), bf16), ((16, columns), bf16)],
        [
            (ANY, block_mask[0]),
            (VMEM, token_rows),
            (VMEM, norm_gain.reshape(1, width)),
        ],
        [pltpu.SMEM((1, n_ctx), jnp.int32), pltpu.SemaphoreType.DMA((1,))],
    )
    x_a = across(packed_a, "tm", 1)
    y_a = across(x_a, "groups", 1)
    shared = w_down.shape[0] * 7 // 16
    sent_down = lax.dynamic_slice_in_dim(w_down, groups * shared, shared, 0)
    sent_down = jnp.concatenate([sent_down, edge], axis=0)
    x_down = across(after(sent_down, packed_a), "tm", 1)

    (near,) = call(
        functools.partial(pack_near_kernel, n_ctx),
        "pack_near",
        [((depth, packed), bf16)],
        [(ANY, w) for w in (packed_a, w_up, w_query, w_key, w_value)],
        [pltpu.SemaphoreType.DMA((4,))],
    )
    block = two_ways(full, (1, 2))
    other_block = across(block, "tp", 1)
    (piece,) = call(split_kernel, "split", [((rows // 2 + 8, width), bf16)], [(VMEM, block)])
    piece = two_ways(piece, (2, 1))
    other_piece = across(piece, "tp", 1)
    sent_out = jnp.concatenate([w_out, w_down[2 * shared :]], axis=0)
    x_out = across(after(sent_out, block), "tm", 1)
    *acts, queries, keys, values, bias = call(
        functools.partial(project_kernel, n_ctx),
        "project",
        [((rows, hidden), bf16)] * n_ctx
        + [((n_ctx * rows, wide), bf16)] * 2
        + [((wide, n_ctx * rows), bf16), ((8 * n_ctx, n_ctx * LANES), f32)],
        [(VMEM, value) for value in (own, block, other_block, piece, other_piece)]
        + [(VMEM, value) for value in (near, x_a, y_a)],
        [
            pltpu.VMEM((n_ctx * rows, width), bf16),
        ],
        flops=2 * n_ctx * rows * width * packed,
        moved=4 << 20,
        transcendentals=n_ctx * rows * hidden,
    )
    parts = [None] * n_ctx
    for blocks in ((2, 3), (1,), (0,)):
        done = call(
            functools.partial(attend_kernel, n_ctx, blocks),
            "attend",
            [((rows, hidden + wide), bf16)] * len(blocks),
            [(VMEM, acts[i]) for i in blocks]
            + [(VMEM, value) for value in (queries, keys, values, bias)],
            flops=4 * len(blocks) * wide * n_ctx * rows * rows,
            transcendentals=len(blocks) * (wide // HEAD_DIM) * n_ctx * rows * rows,
        )
        for i, part in zip(blocks, done):
            parts[i] = part
    y_down = across(after(x_down, near), "groups", 1)
    parts = parts[:1] + [across(parts[i], "ctx", i) for i in range(1, n_ctx)]
    (base,) = call(
        functools.partial(convolve_kernel, dancers_here),
        "convolve",
        [((rows, columns), f32)],
        [
            (VMEM, token_rows),
            (VMEM, mine),
            (VMEM, x_down),
            (VMEM, conv_weight),
            (ANY, x_out),
            (ANY, parts[0]),
        ],
        [pltpu.VMEM((rows + 32, columns), f32)],
        flops=3000000000,
    )
    keep, send = call(
        functools.partial(join_kernel, n_ctx),
        "join",
        [((rows, columns), f32), ((rows, columns), bf16)],
        [(VMEM, w_down), (VMEM, w_out), (VMEM, base)]
        + [(ANY, value) for value in (x_down, y_down, x_out)]
        + [(ANY, value) for value in parts],
        [
            pltpu.VMEM(w_down.shape, bf16),
            pltpu.VMEM(w_out.shape, bf16),
            pltpu.VMEM((rows, w_down.shape[0]), bf16),
            pltpu.VMEM((rows, w_out.shape[0]), bf16),
            pltpu.SemaphoreType.DMA((2 * n_ctx + 4,)),
        ],
        flops=4 * rows * columns * n_ctx * (hidden + wide),
        moved=4 << 20,
    )
    other = across(send, "tp", 1).astype(f32)
    return (keep + other).astype(bf16).reshape(frames_here, dancers_here, columns)


def gather_all(
    tokens, norm_gain, block_mask, w_query, w_key, w_value, w_out, w_up, w_down, conv_weight
):
    frames_here, dancers_here, width = tokens.shape
    rows_here = frames_here * dancers_here
    normed_grid = rms_norm(tokens, norm_gain)
    normed = normed_grid.reshape(rows_here, width)
    query_sum, key_sum, value_sum, hidden = tuple(
        jnp.dot(
            normed,
            lax.all_gather(piece, "tm", axis=0, tiled=True),
            preferred_element_type=jnp.float32,
        )
        for piece in (w_query, w_key, w_value, w_up)
    )
    local_heads = query_sum.shape[1] // HEAD_DIM
    queries = query_sum.astype(jnp.bfloat16).reshape(rows_here, local_heads, HEAD_DIM)
    grid = (frames_here, dancers_here, local_heads * HEAD_DIM)
    key_piece = lax.all_gather(
        key_sum.astype(jnp.bfloat16).reshape(grid), "ctx", axis=1, tiled=True
    )
    value_piece = lax.all_gather(
        value_sum.astype(jnp.bfloat16).reshape(grid), "ctx", axis=1, tiled=True
    )
    count = key_piece.shape[1]
    allowed = jnp.tile(jnp.repeat(block_mask[0, 0].astype(jnp.float32), dancers_here), frames_here)
    key_rows = key_piece.reshape(frames_here * count, local_heads, HEAD_DIM)
    value_rows = value_piece.reshape(frames_here * count, local_heads, HEAD_DIM)
    scores = (
        jnp.einsum("qhd,khd->hqk", queries, key_rows, preferred_element_type=jnp.float32) * 0.125
    )
    scores = jnp.where(allowed[None, None, :] > 0, scores, MASKED)
    expo = jnp.exp(scores - jnp.max(scores, axis=-1, keepdims=True)) * allowed[None, None, :]
    total = jnp.sum(expo, axis=-1)
    mixed = jnp.einsum(
        "hqk,khd->hqd", expo.astype(jnp.bfloat16), value_rows, preferred_element_type=jnp.float32
    )
    attended = (
        (mixed / total[:, :, None])
        .transpose(1, 0, 2)
        .reshape(rows_here, local_heads * HEAD_DIM)
        .astype(jnp.bfloat16)
    )
    activated = jax.nn.gelu(hidden, approximate=True).astype(jnp.bfloat16)
    out_full = lax.all_gather(w_out, "tm", axis=1, tiled=True)
    down_full = lax.all_gather(w_down, "tm", axis=1, tiled=True)
    branches = jnp.dot(attended, out_full, preferred_element_type=jnp.float32)
    branches = branches + jnp.dot(activated, down_full, preferred_element_type=jnp.float32)
    mine = lax.psum_scatter(
        branches.astype(jnp.bfloat16), "tp", scatter_dimension=1, tiled=True
    ).astype(jnp.float32)
    features_here = mine.shape[1]
    first_feature = lax.axis_index("tp") * features_here
    normed_cols = lax.dynamic_slice_in_dim(normed_grid, first_feature, features_here, 2)
    token_cols = lax.dynamic_slice_in_dim(tokens, first_feature, features_here, 2)
    result = (
        token_cols.astype(jnp.float32)
        + mine.reshape(frames_here, dancers_here, features_here)
        + convolve(normed_cols, conv_weight)
    )
    return result.astype(jnp.bfloat16)


def solution(mesh):
    n_ctx, n_tm = mesh.shape["ctx"], mesh.shape["tm"]

    def on_device(*arrays):
        local_heads = arrays[3].shape[1] // HEAD_DIM
        pairs = n_tm == 2 and mesh.shape["groups"] == 2 and mesh.shape["tp"] == 2
        even = n_ctx == 4 and local_heads == 2 * n_ctx
        chosen = split_over_ctx if pairs and even else gather_all
        return chosen(*arrays)

    placed = (
        P(("groups", "tm"), "ctx", None),
        P(),
        P(("groups", "tm"), "ctx", None),
        P("tm", "tp"),
        P("tm", "tp"),
        P("tm", "tp"),
        P("tp", "tm"),
        P("tm", "tp"),
        P("tp", "tm"),
        P(None, "tp"),
    )
    return jax.shard_map(
        on_device,
        mesh=mesh,
        in_specs=placed,
        out_specs=P(("groups", "tm"), "ctx", "tp"),
        check_vma=False,
    )
```

```python
import functools

import jax
import jax.numpy as jnp
from jax import lax
from jax.experimental import pallas as pl
from jax.experimental.pallas import tpu as pltpu
from jax.sharding import PartitionSpec as P

HEAD_DIM = 64
KERNEL = 5
MASKED = -1e30
LANES = 128
AXES = ("ctx", "tm", "groups", "tp")


def from_behind(value, axis, steps):
    count = lax.axis_size(axis)
    first, last = (max(0, -steps), min(count, count - steps))
    return lax.ppermute(value, axis, [(source, source + steps) for source in range(first, last)])


def rms_norm(tokens, norm_gain):
    values = tokens.astype(jnp.float32)
    square = jnp.mean(values * values, axis=-1, keepdims=True)
    return (values * lax.rsqrt(square + 1e-05) * norm_gain).astype(jnp.bfloat16)


def across(value, axis, step):
    count = lax.axis_size(axis)
    return lax.ppermute(value, axis, [(source, source ^ step) for source in range(count)])


def two_ways(value, steps):
    pairs = [
        (2 * source + core, 2 * (source ^ steps[core]) + core)
        for source in range(lax.axis_size("ctx"))
        for core in range(2)
    ]
    return lax.ppermute(value, ("ctx", "tp"), pairs)


def convolve(normed_cols, conv_weight):
    frames_here, dancers_here, features_here = normed_cols.shape
    wide = normed_cols.astype(jnp.float32)
    before = from_behind(normed_cols[frames_here - 2 :], "tm", 1).astype(jnp.float32)
    after = from_behind(normed_cols[0:2], "tm", -1).astype(jnp.float32)
    padded = jnp.concatenate([before, wide, after], axis=0)
    convolved = jnp.zeros((frames_here, dancers_here, features_here), jnp.float32)
    for offset in range(KERNEL):
        convolved = convolved + conv_weight[offset] * padded[offset : offset + frames_here]
    return convolved


def begin(sems, pairs):
    copies = [
        pltpu.make_async_copy(source, target, sems.at[n]) for n, (source, target) in enumerate(pairs)
    ]
    for copy in copies:
        copy.start()
    return copies


def end(copies):
    for copy in copies:
        copy.wait()


def slot(index, size):
    return pl.ds(pl.multiple_of(index * size, size), size)


def dot(left, right):
    return jnp.dot(left, right, preferred_element_type=jnp.float32)


def normalise_kernel(n_ctx, mask_in, tokens, gain, full, own, mine, edge, mask, sems):
    rows, width = tokens.shape
    copies = begin(sems, [(mask_in, mask)])
    values = tokens[...].astype(jnp.float32)
    square = jnp.mean(values * values, axis=-1, keepdims=True)
    full[0:rows, :] = (values * lax.rsqrt(square + 1e-05) * gain[...]).astype(jnp.bfloat16)
    end(copies)
    entries = [
        jnp.full((8, LANES), mask[0, e].astype(jnp.float32), jnp.float32) for e in range(n_ctx)
    ]
    entries.append(jnp.zeros((8, width - n_ctx * LANES), jnp.float32))
    entries = jnp.concatenate(entries, axis=1).astype(jnp.bfloat16)
    full[rows:, :] = entries
    tm, tp = lax.axis_index("tm"), lax.axis_index("tp")
    own[...] = full[...]
    size, columns = edge.shape
    mine[...] = full[0:rows, slot(tp, columns)]
    edge[...] = jnp.where(tm == 0, mine[rows - size :, :], mine[0:size, :])


def pack_kernel(n_ctx, w_up, w_query, w_key, w_value, packed, sems):
    ctx, groups = lax.axis_index("ctx"), lax.axis_index("groups")
    count = packed.shape[0]
    pairs, column = [], 0
    for w in (w_up, w_query, w_key, w_value):
        size = w.shape[1] // n_ctx
        source = w.at[slot(groups, count), slot(ctx, size)]
        pairs.append((source, packed.at[:, column : column + size]))
        column += size
    end(begin(sems, pairs))


def split_kernel(block, piece):
    size = piece.shape[0]
    upper = lax.axis_index("tp") == 1
    piece[...] = jnp.where(upper, block[block.shape[0] - size :, :], block[0:size, :])


def pack_near_kernel(n_ctx, after, w_up, w_query, w_key, w_value, near, sems):
    ctx = lax.axis_index("ctx")
    pairs, column = [], 0
    for w in (w_up, w_query, w_key, w_value):
        size = w.shape[1] // n_ctx
        pairs.append((w.at[:, slot(ctx, size)], near.at[:, column : column + size]))
        column += size
    end(begin(sems, pairs))


def convolve_kernel(per_frame, tokens, mine, received, taps, last0, last1, base, held):
    tm, tp = lax.axis_index("tm"), lax.axis_index("tp")
    rows, columns = base.shape
    edge = 16
    margin = 2 * per_frame
    near = received[received.shape[0] - edge :, :].astype(jnp.float32)
    zeros = jnp.zeros((edge, columns), jnp.float32)
    held[0:edge, :] = jnp.where(tm == 1, near, zeros)
    held[edge : edge + rows, :] = mine[...].astype(jnp.float32)
    held[edge + rows :, :] = jnp.where(tm == 0, near, zeros)
    total = tokens[:, slot(tp, columns)].astype(jnp.float32)
    for offset in range(KERNEL):
        start = edge - margin + offset * per_frame
        total += taps[offset : offset + 1, :] * held[start : start + rows, :]
    base[...] = total


def project_kernel(n_ctx, *refs):
    own, block, other_block, piece, other_piece = refs[:5]
    near, far, farther = refs[5:8]
    acts = refs[8 : 8 + n_ctx]
    queries, keys, values, bias, held = refs[8 + n_ctx :]
    ctx, tm, groups, tp = (lax.axis_index(name) for name in AXES)
    rows, depth = own.shape[0] - 8, near.shape[0]
    sources = (
        (own, slot(0, rows), rows),
        (block, slot(1 + tp, rows), rows),
        (other_block, slot(2 - tp, rows), rows),
        (piece, slot(6 + tp, rows // 2), rows // 2),
        (other_piece, slot(7 - tp, rows // 2), rows // 2),
    )
    half = depth // 2
    cuts = ((0, slot(tm, depth), depth), (depth, slot(2 * (1 - tm) + groups, half), half))
    cuts += ((depth + half, slot(2 * (1 - tm) + 1 - groups, half), half),)
    for source, target, size in sources:
        for to, lanes, wide in cuts:
            held[target, to : to + wide] = source[0:size, lanes]
    total = dot(held[:, 0:depth], near[...])
    total += dot(held[:, depth : depth + half], far[...])
    total += dot(held[:, depth + half :], farther[...])
    hidden, wide = acts[0].shape[1], queries.shape[1]
    activated = jax.nn.gelu(total[:, :hidden], approximate=True).astype(jnp.bfloat16)
    for d in range(n_ctx):
        acts[d][...] = activated[d * rows : (d + 1) * rows]
    projected = total[:, hidden:].astype(jnp.bfloat16)
    queries[...] = projected[:, 0:wide]
    keys[...] = projected[:, wide : 2 * wide]
    values[...] = projected[:, 2 * wide :].T
    for j in range(n_ctx):
        lanes = slot(ctx ^ j, LANES)
        one, other = block[rows:, lanes], other_block[rows:, lanes]
        last, other_last = piece[rows // 2 :, lanes], other_piece[rows // 2 :, lanes]
        entries = (
            own[rows:, lanes],
            jnp.where(tp == 0, one, other),
            jnp.where(tp == 0, other, one),
            jnp.where(tp == 0, other_last, last),
        )
        for i, entry in enumerate(entries):
            flag = entry.astype(jnp.float32)
            target = slice(j * LANES, (j + 1) * LANES)
            bias[8 * i : 8 * (i + 1), target] = jnp.where(flag > 0, 0.0, MASKED)


def attend_kernel(n_ctx, blocks, *refs):
    count = len(blocks)
    acts, (queries, keys, values, bias) = refs[:count], refs[count : count + 4]
    outs = refs[count + 4 :]
    rows, hidden = acts[0].shape
    wide = outs[0].shape[1] - hidden
    lane_head = lax.broadcasted_iota(jnp.int32, (1, wide), 1) // HEAD_DIM
    for n, i in enumerate(blocks):
        block = queries[i * rows : (i + 1) * rows, :]
        allowed = jnp.concatenate(
            [
                jnp.broadcast_to(
                    bias[8 * i : 8 * i + 1, j * LANES : (j + 1) * LANES], (rows, rows)
                )
                for j in range(n_ctx)
            ],
            axis=0,
        )
        results = []
        for head in range(wide // HEAD_DIM):
            one = jnp.where(lane_head == head, block, jnp.zeros_like(block))
            scores = lax.dot_general(
                keys[...], one, (((1,), (1,)), ((), ())), preferred_element_type=jnp.float32
            )
            scores = scores * 0.125 + allowed
            peak = jnp.max(scores, axis=0, keepdims=True)
            expo = jnp.exp(scores - peak)
            total = jnp.sum(expo, axis=0, keepdims=True)
            mixed = dot(
                values[head * HEAD_DIM : (head + 1) * HEAD_DIM, :], expo.astype(jnp.bfloat16)
            )
            results.append(mixed / total)
        outs[n][:, 0:hidden] = acts[n][...]
        outs[n][:, hidden:] = jnp.concatenate(results, axis=0).T.astype(jnp.bfloat16)


def join_kernel(n_ctx, *refs):
    near_down, near_out, base = refs[:3]
    far_down, farther_down, far_out = refs[3:6]
    parts = refs[6 : 6 + n_ctx]
    keep, send, down, acts, atts = refs[6 + n_ctx :]
    ctx, tm, groups, tp = (lax.axis_index(name) for name in AXES)
    hidden, wide = acts.shape[1] // n_ctx, atts.shape[1] // n_ctx
    count, depth = farther_down.shape[0] - 16, near_out.shape[0]
    down[slot(groups, count), :] = far_down[0:count, :]
    down[slot(1 - groups, count), :] = farther_down[0:count, :]
    down[2 * count :, :] = far_out[depth:, :]
    for d in range(n_ctx):
        acts[:, slot(ctx ^ d, hidden)] = parts[d][:, 0:hidden]
        atts[:, slot(ctx ^ d, wide)] = parts[d][:, hidden:]
    near_sum = dot(acts[...], near_down[...]) + dot(atts[...], near_out[...])
    far_sum = dot(acts[...], down[...]) + dot(atts[...], far_out[0:depth, :])
    same = tm == tp
    keep[...] = jnp.where(same, near_sum, far_sum) + base[...]
    send[...] = jnp.where(same, far_sum, near_sum).astype(jnp.bfloat16)


SMEM = pl.BlockSpec(memory_space=pltpu.SMEM)
VMEM = pl.BlockSpec(memory_space=pltpu.VMEM)
ANY = pl.BlockSpec(memory_space=pl.ANY)


def call(
    kernel, name, outs, ins, scratch=(), flops=0, moved=1 << 20, transcendentals=0, limit=8 << 20
):
    specs, values = zip(*ins)
    return pl.pallas_call(
        kernel,
        out_shape=[jax.ShapeDtypeStruct(shape, dtype) for shape, dtype in outs],
        in_specs=list(specs),
        out_specs=[VMEM] * len(outs),
        scratch_shapes=list(scratch),
        compiler_params=pltpu.CompilerParams(vmem_limit_bytes=limit),
        name=name,
        cost_estimate=pl.CostEstimate(
            flops=flops, bytes_accessed=moved, transcendentals=transcendentals
        ),
    )(*values)


def after(value, *others):
    return lax.optimization_barrier((value, others))[0]


def split_over_ctx(
    tokens, norm_gain, block_mask, w_query, w_key, w_value, w_out, w_up, w_down, conv_weight
):
    n_ctx = lax.axis_size("ctx")
    groups, ctx = lax.axis_index("groups"), lax.axis_index("ctx")
    tm, tp = lax.axis_index("tm"), lax.axis_index("tp")
    frames_here, dancers_here, width = tokens.shape
    rows = frames_here * dancers_here
    depth = w_query.shape[0]
    wide = w_query.shape[1] // n_ctx
    hidden = w_up.shape[1] // n_ctx
    columns = w_out.shape[1]
    packed = hidden + 3 * wide
    bf16, f32 = jnp.bfloat16, jnp.float32
    (packed_a,) = call(
        functools.partial(pack_kernel, n_ctx),
        "pack",
        [((depth // 2, packed), bf16)],
        [(ANY, w) for w in (w_up, w_query, w_key, w_value)],
        [pltpu.SemaphoreType.DMA((4,))],
        limit=(54 << 20) - (700 << 10),
    )
    token_rows = after(tokens, packed_a).reshape(rows, width)
    full, own, mine, edge = call(
        functools.partial(normalise_kernel, n_ctx),
        "normalise",
        [((rows + 8, width), bf16)] * 2 + [((rows, columns), bf16), ((16, columns), bf16)],
        [
            (ANY, block_mask[0]),
            (VMEM, token_rows),
            (VMEM, norm_gain.reshape(1, width)),
        ],
        [pltpu.SMEM((1, n_ctx), jnp.int32), pltpu.SemaphoreType.DMA((1,))],
    )
    x_a = across(packed_a, "tm", 1)
    y_a = across(x_a, "groups", 1)
    shared = w_down.shape[0] * 7 // 16
    sent_down = lax.dynamic_slice_in_dim(w_down, groups * shared, shared, 0)
    sent_down = jnp.concatenate([sent_down, edge], axis=0)
    x_down = across(after(sent_down, packed_a), "tm", 1)

    (near,) = call(
        functools.partial(pack_near_kernel, n_ctx),
        "pack_near",
        [((depth, packed), bf16)],
        [(ANY, w) for w in (packed_a, w_up, w_query, w_key, w_value)],
        [pltpu.SemaphoreType.DMA((4,))],
    )
    block = two_ways(full, (1, 2))
    other_block = across(block, "tp", 1)
    (piece,) = call(split_kernel, "split", [((rows // 2 + 8, width), bf16)], [(VMEM, block)])
    piece = two_ways(piece, (2, 1))
    other_piece = across(piece, "tp", 1)
    sent_out = jnp.concatenate([w_out, w_down[2 * shared :]], axis=0)
    x_out = across(after(sent_out, block), "tm", 1)
    *acts, queries, keys, values, bias = call(
        functools.partial(project_kernel, n_ctx),
        "project",
        [((rows, hidden), bf16)] * n_ctx
        + [((n_ctx * rows, wide), bf16)] * 2
        + [((wide, n_ctx * rows), bf16), ((8 * n_ctx, n_ctx * LANES), f32)],
        [(VMEM, value) for value in (own, block, other_block, piece, other_piece)]
        + [(VMEM, value) for value in (near, x_a, y_a)],
        [
            pltpu.VMEM((n_ctx * rows, width), bf16),
        ],
        flops=2 * n_ctx * rows * width * packed,
        moved=4 << 20,
        transcendentals=n_ctx * rows * hidden,
    )
    parts = [None] * n_ctx
    for blocks in ((2, 3), (1,), (0,)):
        done = call(
            functools.partial(attend_kernel, n_ctx, blocks),
            "attend",
            [((rows, hidden + wide), bf16)] * len(blocks),
            [(VMEM, acts[i]) for i in blocks]
            + [(VMEM, value) for value in (queries, keys, values, bias)],
            flops=4 * len(blocks) * wide * n_ctx * rows * rows,
            transcendentals=len(blocks) * (wide // HEAD_DIM) * n_ctx * rows * rows,
        )
        for i, part in zip(blocks, done):
            parts[i] = part
    y_down = across(after(x_down, near), "groups", 1)
    parts = parts[:1] + [across(parts[i], "ctx", i) for i in range(1, n_ctx)]
    (base,) = call(
        functools.partial(convolve_kernel, dancers_here),
        "convolve",
        [((rows, columns), f32)],
        [
            (VMEM, token_rows),
            (VMEM, mine),
            (VMEM, x_down),
            (VMEM, conv_weight),
            (ANY, x_out),
            (ANY, parts[0]),
        ],
        [pltpu.VMEM((rows + 32, columns), f32)],
        flops=3000000000,
    )
    keep, send = call(
        functools.partial(join_kernel, n_ctx),
        "join",
        [((rows, columns), f32), ((rows, columns), bf16)],
        [(VMEM, w_down), (VMEM, w_out), (VMEM, base)]
        + [(VMEM, value) for value in (x_down, y_down, x_out)]
        + [(VMEM, value) for value in parts],
        [
            pltpu.VMEM(w_down.shape, bf16),
            pltpu.VMEM((rows, w_down.shape[0]), bf16),
            pltpu.VMEM((rows, w_out.shape[0]), bf16),
        ],
        flops=4 * rows * columns * n_ctx * (hidden + wide),
        moved=4 << 20,
    )
    other = across(send, "tp", 1).astype(f32)
    return (keep + other).astype(bf16).reshape(frames_here, dancers_here, columns)


def gather_all(
    tokens, norm_gain, block_mask, w_query, w_key, w_value, w_out, w_up, w_down, conv_weight
):
    frames_here, dancers_here, width = tokens.shape
    rows_here = frames_here * dancers_here
    normed_grid = rms_norm(tokens, norm_gain)
    normed = normed_grid.reshape(rows_here, width)
    query_sum, key_sum, value_sum, hidden = tuple(
        jnp.dot(
            normed,
            lax.all_gather(piece, "tm", axis=0, tiled=True),
            preferred_element_type=jnp.float32,
        )
        for piece in (w_query, w_key, w_value, w_up)
    )
    local_heads = query_sum.shape[1] // HEAD_DIM
    queries = query_sum.astype(jnp.bfloat16).reshape(rows_here, local_heads, HEAD_DIM)
    grid = (frames_here, dancers_here, local_heads * HEAD_DIM)
    key_piece = lax.all_gather(
        key_sum.astype(jnp.bfloat16).reshape(grid), "ctx", axis=1, tiled=True
    )
    value_piece = lax.all_gather(
        value_sum.astype(jnp.bfloat16).reshape(grid), "ctx", axis=1, tiled=True
    )
    count = key_piece.shape[1]
    allowed = jnp.tile(jnp.repeat(block_mask[0, 0].astype(jnp.float32), dancers_here), frames_here)
    key_rows = key_piece.reshape(frames_here * count, local_heads, HEAD_DIM)
    value_rows = value_piece.reshape(frames_here * count, local_heads, HEAD_DIM)
    scores = (
        jnp.einsum("qhd,khd->hqk", queries, key_rows, preferred_element_type=jnp.float32) * 0.125
    )
    scores = jnp.where(allowed[None, None, :] > 0, scores, MASKED)
    expo = jnp.exp(scores - jnp.max(scores, axis=-1, keepdims=True)) * allowed[None, None, :]
    total = jnp.sum(expo, axis=-1)
    mixed = jnp.einsum(
        "hqk,khd->hqd", expo.astype(jnp.bfloat16), value_rows, preferred_element_type=jnp.float32
    )
    attended = (
        (mixed / total[:, :, None])
        .transpose(1, 0, 2)
        .reshape(rows_here, local_heads * HEAD_DIM)
        .astype(jnp.bfloat16)
    )
    activated = jax.nn.gelu(hidden, approximate=True).astype(jnp.bfloat16)
    out_full = lax.all_gather(w_out, "tm", axis=1, tiled=True)
    down_full = lax.all_gather(w_down, "tm", axis=1, tiled=True)
    branches = jnp.dot(attended, out_full, preferred_element_type=jnp.float32)
    branches = branches + jnp.dot(activated, down_full, preferred_element_type=jnp.float32)
    mine = lax.psum_scatter(
        branches.astype(jnp.bfloat16), "tp", scatter_dimension=1, tiled=True
    ).astype(jnp.float32)
    features_here = mine.shape[1]
    first_feature = lax.axis_index("tp") * features_here
    normed_cols = lax.dynamic_slice_in_dim(normed_grid, first_feature, features_here, 2)
    token_cols = lax.dynamic_slice_in_dim(tokens, first_feature, features_here, 2)
    result = (
        token_cols.astype(jnp.float32)
        + mine.reshape(frames_here, dancers_here, features_here)
        + convolve(normed_cols, conv_weight)
    )
    return result.astype(jnp.bfloat16)


def solution(mesh):
    n_ctx, n_tm = mesh.shape["ctx"], mesh.shape["tm"]

    def on_device(*arrays):
        local_heads = arrays[3].shape[1] // HEAD_DIM
        pairs = n_tm == 2 and mesh.shape["groups"] == 2 and mesh.shape["tp"] == 2
        even = n_ctx == 4 and local_heads == 2 * n_ctx
        chosen = split_over_ctx if pairs and even else gather_all
        return chosen(*arrays)

    placed = (
        P(("groups", "tm"), "ctx", None),
        P(),
        P(("groups", "tm"), "ctx", None),
        P("tm", "tp"),
        P("tm", "tp"),
        P("tm", "tp"),
        P("tp", "tm"),
        P("tm", "tp"),
        P("tp", "tm"),
        P(None, "tp"),
    )
    return jax.shard_map(
        on_device,
        mesh=mesh,
        in_specs=placed,
        out_specs=P(("groups", "tm"), "ctx", "tp"),
        check_vma=False,
    )
```

```python
import functools

import jax
import jax.numpy as jnp
from jax import lax
from jax.experimental import pallas as pl
from jax.experimental.pallas import tpu as pltpu
from jax.sharding import PartitionSpec as P

HEAD_DIM = 64
KERNEL = 5
MASKED = -1e30
LANES = 128
AXES = ("ctx", "tm", "groups", "tp")


def from_behind(value, axis, steps):
    count = lax.axis_size(axis)
    first, last = (max(0, -steps), min(count, count - steps))
    return lax.ppermute(value, axis, [(source, source + steps) for source in range(first, last)])


def rms_norm(tokens, norm_gain):
    values = tokens.astype(jnp.float32)
    square = jnp.mean(values * values, axis=-1, keepdims=True)
    return (values * lax.rsqrt(square + 1e-05) * norm_gain).astype(jnp.bfloat16)


def across(value, axis, step):
    count = lax.axis_size(axis)
    return lax.ppermute(value, axis, [(source, source ^ step) for source in range(count)])


def two_ways(value, steps):
    pairs = [
        (2 * source + core, 2 * (source ^ steps[core]) + core)
        for source in range(lax.axis_size("ctx"))
        for core in range(2)
    ]
    return lax.ppermute(value, ("ctx", "tp"), pairs)


def convolve(normed_cols, conv_weight):
    frames_here, dancers_here, features_here = normed_cols.shape
    wide = normed_cols.astype(jnp.float32)
    before = from_behind(normed_cols[frames_here - 2 :], "tm", 1).astype(jnp.float32)
    after = from_behind(normed_cols[0:2], "tm", -1).astype(jnp.float32)
    padded = jnp.concatenate([before, wide, after], axis=0)
    convolved = jnp.zeros((frames_here, dancers_here, features_here), jnp.float32)
    for offset in range(KERNEL):
        convolved = convolved + conv_weight[offset] * padded[offset : offset + frames_here]
    return convolved


def begin(sems, pairs):
    copies = [
        pltpu.make_async_copy(source, target, sems.at[n]) for n, (source, target) in enumerate(pairs)
    ]
    for copy in copies:
        copy.start()
    return copies


def end(copies):
    for copy in copies:
        copy.wait()


def slot(index, size):
    return pl.ds(pl.multiple_of(index * size, size), size)


def dot(left, right):
    return jnp.dot(left, right, preferred_element_type=jnp.float32)


def normalise_kernel(n_ctx, mask_in, tokens, gain, full, own, mine, edge, mask, sems):
    rows, width = tokens.shape
    copies = begin(sems, [(mask_in, mask)])
    values = tokens[...].astype(jnp.float32)
    square = jnp.mean(values * values, axis=-1, keepdims=True)
    full[0:rows, :] = (values * lax.rsqrt(square + 1e-05) * gain[...]).astype(jnp.bfloat16)
    end(copies)
    entries = [
        jnp.full((8, LANES), mask[0, e].astype(jnp.float32), jnp.float32) for e in range(n_ctx)
    ]
    entries.append(jnp.zeros((8, width - n_ctx * LANES), jnp.float32))
    entries = jnp.concatenate(entries, axis=1).astype(jnp.bfloat16)
    full[rows:, :] = entries
    tm, tp = lax.axis_index("tm"), lax.axis_index("tp")
    own[...] = full[...]
    size, columns = edge.shape
    mine[...] = full[0:rows, slot(tp, columns)]
    edge[...] = jnp.where(tm == 0, mine[rows - size :, :], mine[0:size, :])


def pack_kernel(n_ctx, w_up, w_query, w_key, w_value, packed, sems):
    ctx, groups = lax.axis_index("ctx"), lax.axis_index("groups")
    count = packed.shape[0]
    pairs, column = [], 0
    for w in (w_up, w_query, w_key, w_value):
        size = w.shape[1] // n_ctx
        source = w.at[slot(groups, count), slot(ctx, size)]
        pairs.append((source, packed.at[:, column : column + size]))
        column += size
    end(begin(sems, pairs))


def split_kernel(block, piece):
    size = piece.shape[0]
    upper = lax.axis_index("tp") == 1
    piece[...] = jnp.where(upper, block[block.shape[0] - size :, :], block[0:size, :])


def pack_near_kernel(n_ctx, after, w_up, w_query, w_key, w_value, near, sems):
    ctx = lax.axis_index("ctx")
    pairs, column = [], 0
    for w in (w_up, w_query, w_key, w_value):
        size = w.shape[1] // n_ctx
        pairs.append((w.at[:, slot(ctx, size)], near.at[:, column : column + size]))
        column += size
    end(begin(sems, pairs))


def convolve_kernel(per_frame, tokens, mine, received, taps, last0, last1, base, held):
    tm, tp = lax.axis_index("tm"), lax.axis_index("tp")
    rows, columns = base.shape
    edge = 16
    margin = 2 * per_frame
    near = received[received.shape[0] - edge :, :].astype(jnp.float32)
    zeros = jnp.zeros((edge, columns), jnp.float32)
    held[0:edge, :] = jnp.where(tm == 1, near, zeros)
    held[edge : edge + rows, :] = mine[...].astype(jnp.float32)
    held[edge + rows :, :] = jnp.where(tm == 0, near, zeros)
    total = tokens[:, slot(tp, columns)].astype(jnp.float32)
    for offset in range(KERNEL):
        start = edge - margin + offset * per_frame
        total += taps[offset : offset + 1, :] * held[start : start + rows, :]
    base[...] = total


def project_kernel(n_ctx, *refs):
    own, block, other_block, piece, other_piece = refs[:5]
    near, far, farther = refs[5:8]
    acts = refs[8 : 8 + n_ctx]
    queries, keys, values, bias, held = refs[8 + n_ctx :]
    ctx, tm, groups, tp = (lax.axis_index(name) for name in AXES)
    rows, depth = own.shape[0] - 8, near.shape[0]
    sources = (
        (own, slot(0, rows), rows),
        (block, slot(1 + tp, rows), rows),
        (other_block, slot(2 - tp, rows), rows),
        (piece, slot(6 + tp, rows // 2), rows // 2),
        (other_piece, slot(7 - tp, rows // 2), rows // 2),
    )
    half = depth // 2
    cuts = ((0, slot(tm, depth), depth), (depth, slot(2 * (1 - tm) + groups, half), half))
    cuts += ((depth + half, slot(2 * (1 - tm) + 1 - groups, half), half),)
    for source, target, size in sources:
        for to, lanes, wide in cuts:
            held[target, to : to + wide] = source[0:size, lanes]
    total = dot(held[:, 0:depth], near[...])
    total += dot(held[:, depth : depth + half], far[...])
    total += dot(held[:, depth + half :], farther[...])
    hidden, wide = acts[0].shape[1], queries.shape[1]
    activated = jax.nn.gelu(total[:, :hidden], approximate=True).astype(jnp.bfloat16)
    for d in range(n_ctx):
        acts[d][...] = activated[d * rows : (d + 1) * rows]
    projected = total[:, hidden:].astype(jnp.bfloat16)
    queries[...] = projected[:, 0:wide]
    keys[...] = projected[:, wide : 2 * wide]
    values[...] = projected[:, 2 * wide :].T
    for j in range(n_ctx):
        lanes = slot(ctx ^ j, LANES)
        one, other = block[rows:, lanes], other_block[rows:, lanes]
        last, other_last = piece[rows // 2 :, lanes], other_piece[rows // 2 :, lanes]
        entries = (
            own[rows:, lanes],
            jnp.where(tp == 0, one, other),
            jnp.where(tp == 0, other, one),
            jnp.where(tp == 0, other_last, last),
        )
        for i, entry in enumerate(entries):
            flag = entry.astype(jnp.float32)
            target = slice(j * LANES, (j + 1) * LANES)
            bias[8 * i : 8 * (i + 1), target] = jnp.where(flag > 0, 0.0, MASKED)


def attend_kernel(n_ctx, blocks, *refs):
    count = len(blocks)
    acts, (queries, keys, values, bias) = refs[:count], refs[count : count + 4]
    outs = refs[count + 4 :]
    rows, hidden = acts[0].shape
    wide = outs[0].shape[1] - hidden
    lane_head = lax.broadcasted_iota(jnp.int32, (1, wide), 1) // HEAD_DIM
    for n, i in enumerate(blocks):
        block = queries[i * rows : (i + 1) * rows, :]
        allowed = jnp.concatenate(
            [
                jnp.broadcast_to(
                    bias[8 * i : 8 * i + 1, j * LANES : (j + 1) * LANES], (rows, rows)
                )
                for j in range(n_ctx)
            ],
            axis=0,
        )
        results = []
        for head in range(wide // HEAD_DIM):
            one = jnp.where(lane_head == head, block, jnp.zeros_like(block))
            scores = lax.dot_general(
                keys[...], one, (((1,), (1,)), ((), ())), preferred_element_type=jnp.float32
            )
            scores = scores * 0.125 + allowed
            peak = jnp.max(scores, axis=0, keepdims=True)
            expo = jnp.exp(scores - peak)
            total = jnp.sum(expo, axis=0, keepdims=True)
            mixed = dot(
                values[head * HEAD_DIM : (head + 1) * HEAD_DIM, :], expo.astype(jnp.bfloat16)
            )
            results.append(mixed / total)
        outs[n][:, 0:hidden] = acts[n][...]
        outs[n][:, hidden:] = jnp.concatenate(results, axis=0).T.astype(jnp.bfloat16)


def join_kernel(n_ctx, *refs):
    near_down, near_out, base = refs[:3]
    far_down, farther_down, far_out = refs[3:6]
    parts = refs[6 : 6 + n_ctx]
    keep, send, down, acts, atts = refs[6 + n_ctx :]
    ctx, tm, groups, tp = (lax.axis_index(name) for name in AXES)
    hidden, wide = acts.shape[1] // n_ctx, atts.shape[1] // n_ctx
    count, depth = farther_down.shape[0] - 16, near_out.shape[0]
    down[slot(groups, count), :] = far_down[0:count, :]
    down[slot(1 - groups, count), :] = farther_down[0:count, :]
    down[2 * count :, :] = far_out[depth:, :]
    for d in range(n_ctx):
        acts[:, slot(ctx ^ d, hidden)] = parts[d][:, 0:hidden]
        atts[:, slot(ctx ^ d, wide)] = parts[d][:, hidden:]
    near_sum = dot(acts[...], near_down[...]) + dot(atts[...], near_out[...])
    far_sum = dot(acts[...], down[...]) + dot(atts[...], far_out[0:depth, :])
    same = tm == tp
    keep[...] = jnp.where(same, near_sum, far_sum) + base[...]
    send[...] = jnp.where(same, far_sum, near_sum).astype(jnp.bfloat16)


def finish_kernel(keep, other, out):
    total = keep[...] + other[...].astype(jnp.float32)
    out[...] = total.reshape(out.shape).astype(jnp.bfloat16)


SMEM = pl.BlockSpec(memory_space=pltpu.SMEM)
VMEM = pl.BlockSpec(memory_space=pltpu.VMEM)
ANY = pl.BlockSpec(memory_space=pl.ANY)


def call(
    kernel, name, outs, ins, scratch=(), flops=0, moved=1 << 20, transcendentals=0, limit=8 << 20
):
    specs, values = zip(*ins)
    return pl.pallas_call(
        kernel,
        out_shape=[jax.ShapeDtypeStruct(shape, dtype) for shape, dtype in outs],
        in_specs=list(specs),
        out_specs=[VMEM] * len(outs),
        scratch_shapes=list(scratch),
        compiler_params=pltpu.CompilerParams(vmem_limit_bytes=limit),
        name=name,
        cost_estimate=pl.CostEstimate(
            flops=flops, bytes_accessed=moved, transcendentals=transcendentals
        ),
    )(*values)


def after(value, *others):
    return lax.optimization_barrier((value, others))[0]


def split_over_ctx(
    tokens, norm_gain, block_mask, w_query, w_key, w_value, w_out, w_up, w_down, conv_weight
):
    n_ctx = lax.axis_size("ctx")
    groups, ctx = lax.axis_index("groups"), lax.axis_index("ctx")
    tm, tp = lax.axis_index("tm"), lax.axis_index("tp")
    frames_here, dancers_here, width = tokens.shape
    rows = frames_here * dancers_here
    depth = w_query.shape[0]
    wide = w_query.shape[1] // n_ctx
    hidden = w_up.shape[1] // n_ctx
    columns = w_out.shape[1]
    packed = hidden + 3 * wide
    bf16, f32 = jnp.bfloat16, jnp.float32
    (packed_a,) = call(
        functools.partial(pack_kernel, n_ctx),
        "pack",
        [((depth // 2, packed), bf16)],
        [(ANY, w) for w in (w_up, w_query, w_key, w_value)],
        [pltpu.SemaphoreType.DMA((4,))],
        limit=(54 << 20) - (700 << 10),
    )
    token_rows = after(tokens, packed_a).reshape(rows, width)
    full, own, mine, edge = call(
        functools.partial(normalise_kernel, n_ctx),
        "normalise",
        [((rows + 8, width), bf16)] * 2 + [((rows, columns), bf16), ((16, columns), bf16)],
        [
            (ANY, block_mask[0]),
            (VMEM, token_rows),
            (VMEM, norm_gain.reshape(1, width)),
        ],
        [pltpu.SMEM((1, n_ctx), jnp.int32), pltpu.SemaphoreType.DMA((1,))],
    )
    x_a = across(packed_a, "tm", 1)
    y_a = across(x_a, "groups", 1)
    shared = w_down.shape[0] * 7 // 16
    sent_down = lax.dynamic_slice_in_dim(w_down, groups * shared, shared, 0)
    sent_down = jnp.concatenate([sent_down, edge], axis=0)
    x_down = across(after(sent_down, packed_a), "tm", 1)

    (near,) = call(
        functools.partial(pack_near_kernel, n_ctx),
        "pack_near",
        [((depth, packed), bf16)],
        [(ANY, w) for w in (packed_a, w_up, w_query, w_key, w_value)],
        [pltpu.SemaphoreType.DMA((4,))],
    )
    block = two_ways(full, (1, 2))
    other_block = across(block, "tp", 1)
    (piece,) = call(split_kernel, "split", [((rows // 2 + 8, width), bf16)], [(VMEM, block)])
    piece = two_ways(piece, (2, 1))
    other_piece = across(piece, "tp", 1)
    sent_out = jnp.concatenate([w_out, w_down[2 * shared :]], axis=0)
    x_out = across(after(sent_out, block), "tm", 1)
    *acts, queries, keys, values, bias = call(
        functools.partial(project_kernel, n_ctx),
        "project",
        [((rows, hidden), bf16)] * n_ctx
        + [((n_ctx * rows, wide), bf16)] * 2
        + [((wide, n_ctx * rows), bf16), ((8 * n_ctx, n_ctx * LANES), f32)],
        [(VMEM, value) for value in (own, block, other_block, piece, other_piece)]
        + [(VMEM, value) for value in (near, x_a, y_a)],
        [
            pltpu.VMEM((n_ctx * rows, width), bf16),
        ],
        flops=2 * n_ctx * rows * width * packed,
        moved=4 << 20,
        transcendentals=n_ctx * rows * hidden,
    )
    parts = [None] * n_ctx
    for blocks in ((2, 3), (1,), (0,)):
        done = call(
            functools.partial(attend_kernel, n_ctx, blocks),
            "attend",
            [((rows, hidden + wide), bf16)] * len(blocks),
            [(VMEM, acts[i]) for i in blocks]
            + [(VMEM, value) for value in (queries, keys, values, bias)],
            flops=4 * len(blocks) * wide * n_ctx * rows * rows,
            transcendentals=len(blocks) * (wide // HEAD_DIM) * n_ctx * rows * rows,
        )
        for i, part in zip(blocks, done):
            parts[i] = part
    y_down = across(after(x_down, near), "groups", 1)
    parts = parts[:1] + [across(parts[i], "ctx", i) for i in range(1, n_ctx)]
    (base,) = call(
        functools.partial(convolve_kernel, dancers_here),
        "convolve",
        [((rows, columns), f32)],
        [
            (VMEM, token_rows),
            (VMEM, mine),
            (VMEM, x_down),
            (VMEM, conv_weight),
            (ANY, x_out),
            (ANY, parts[0]),
        ],
        [pltpu.VMEM((rows + 32, columns), f32)],
        flops=3000000000,
    )
    keep, send = call(
        functools.partial(join_kernel, n_ctx),
        "join",
        [((rows, columns), f32), ((rows, columns), bf16)],
        [(VMEM, w_down), (VMEM, w_out), (VMEM, base)]
        + [(VMEM, value) for value in (x_down, y_down, x_out)]
        + [(VMEM, value) for value in parts],
        [
            pltpu.VMEM(w_down.shape, bf16),
            pltpu.VMEM((rows, w_down.shape[0]), bf16),
            pltpu.VMEM((rows, w_out.shape[0]), bf16),
        ],
        flops=4 * rows * columns * n_ctx * (hidden + wide),
        moved=4 << 20,
    )
    other = across(send, "tp", 1)
    (denoised,) = call(
        finish_kernel,
        "finish",
        [((frames_here, dancers_here, columns), bf16)],
        [(VMEM, keep), (VMEM, other)],
    )
    return denoised


def gather_all(
    tokens, norm_gain, block_mask, w_query, w_key, w_value, w_out, w_up, w_down, conv_weight
):
    frames_here, dancers_here, width = tokens.shape
    rows_here = frames_here * dancers_here
    normed_grid = rms_norm(tokens, norm_gain)
    normed = normed_grid.reshape(rows_here, width)
    query_sum, key_sum, value_sum, hidden = tuple(
        jnp.dot(
            normed,
            lax.all_gather(piece, "tm", axis=0, tiled=True),
            preferred_element_type=jnp.float32,
        )
        for piece in (w_query, w_key, w_value, w_up)
    )
    local_heads = query_sum.shape[1] // HEAD_DIM
    queries = query_sum.astype(jnp.bfloat16).reshape(rows_here, local_heads, HEAD_DIM)
    grid = (frames_here, dancers_here, local_heads * HEAD_DIM)
    key_piece = lax.all_gather(
        key_sum.astype(jnp.bfloat16).reshape(grid), "ctx", axis=1, tiled=True
    )
    value_piece = lax.all_gather(
        value_sum.astype(jnp.bfloat16).reshape(grid), "ctx", axis=1, tiled=True
    )
    count = key_piece.shape[1]
    allowed = jnp.tile(jnp.repeat(block_mask[0, 0].astype(jnp.float32), dancers_here), frames_here)
    key_rows = key_piece.reshape(frames_here * count, local_heads, HEAD_DIM)
    value_rows = value_piece.reshape(frames_here * count, local_heads, HEAD_DIM)
    scores = (
        jnp.einsum("qhd,khd->hqk", queries, key_rows, preferred_element_type=jnp.float32) * 0.125
    )
    scores = jnp.where(allowed[None, None, :] > 0, scores, MASKED)
    expo = jnp.exp(scores - jnp.max(scores, axis=-1, keepdims=True)) * allowed[None, None, :]
    total = jnp.sum(expo, axis=-1)
    mixed = jnp.einsum(
        "hqk,khd->hqd", expo.astype(jnp.bfloat16), value_rows, preferred_element_type=jnp.float32
    )
    attended = (
        (mixed / total[:, :, None])
        .transpose(1, 0, 2)
        .reshape(rows_here, local_heads * HEAD_DIM)
        .astype(jnp.bfloat16)
    )
    activated = jax.nn.gelu(hidden, approximate=True).astype(jnp.bfloat16)
    out_full = lax.all_gather(w_out, "tm", axis=1, tiled=True)
    down_full = lax.all_gather(w_down, "tm", axis=1, tiled=True)
    branches = jnp.dot(attended, out_full, preferred_element_type=jnp.float32)
    branches = branches + jnp.dot(activated, down_full, preferred_element_type=jnp.float32)
    mine = lax.psum_scatter(
        branches.astype(jnp.bfloat16), "tp", scatter_dimension=1, tiled=True
    ).astype(jnp.float32)
    features_here = mine.shape[1]
    first_feature = lax.axis_index("tp") * features_here
    normed_cols = lax.dynamic_slice_in_dim(normed_grid, first_feature, features_here, 2)
    token_cols = lax.dynamic_slice_in_dim(tokens, first_feature, features_here, 2)
    result = (
        token_cols.astype(jnp.float32)
        + mine.reshape(frames_here, dancers_here, features_here)
        + convolve(normed_cols, conv_weight)
    )
    return result.astype(jnp.bfloat16)


def solution(mesh):
    n_ctx, n_tm = mesh.shape["ctx"], mesh.shape["tm"]

    def on_device(*arrays):
        local_heads = arrays[3].shape[1] // HEAD_DIM
        pairs = n_tm == 2 and mesh.shape["groups"] == 2 and mesh.shape["tp"] == 2
        even = n_ctx == 4 and local_heads == 2 * n_ctx
        chosen = split_over_ctx if pairs and even else gather_all
        return chosen(*arrays)

    placed = (
        P(("groups", "tm"), "ctx", None),
        P(),
        P(("groups", "tm"), "ctx", None),
        P("tm", "tp"),
        P("tm", "tp"),
        P("tm", "tp"),
        P("tp", "tm"),
        P("tm", "tp"),
        P("tp", "tm"),
        P(None, "tp"),
    )
    return jax.shard_map(
        on_device,
        mesh=mesh,
        in_specs=placed,
        out_specs=P(("groups", "tm"), "ctx", "tp"),
        check_vma=False,
    )
```

```python
import functools

import jax
import jax.numpy as jnp
from jax import lax
from jax.experimental import pallas as pl
from jax.experimental.pallas import tpu as pltpu
from jax.sharding import PartitionSpec as P

HEAD_DIM = 64
KERNEL = 5
MASKED = -1e30
LANES = 128
AXES = ("ctx", "tm", "groups", "tp")


def from_behind(value, axis, steps):
    count = lax.axis_size(axis)
    first, last = (max(0, -steps), min(count, count - steps))
    return lax.ppermute(value, axis, [(source, source + steps) for source in range(first, last)])


def rms_norm(tokens, norm_gain):
    values = tokens.astype(jnp.float32)
    square = jnp.mean(values * values, axis=-1, keepdims=True)
    return (values * lax.rsqrt(square + 1e-05) * norm_gain).astype(jnp.bfloat16)


def across(value, axis, step):
    count = lax.axis_size(axis)
    return lax.ppermute(value, axis, [(source, source ^ step) for source in range(count)])


def two_ways(value, steps):
    pairs = [
        (2 * source + core, 2 * (source ^ steps[core]) + core)
        for source in range(lax.axis_size("ctx"))
        for core in range(2)
    ]
    return lax.ppermute(value, ("ctx", "tp"), pairs)


def convolve(normed_cols, conv_weight):
    frames_here, dancers_here, features_here = normed_cols.shape
    wide = normed_cols.astype(jnp.float32)
    before = from_behind(normed_cols[frames_here - 2 :], "tm", 1).astype(jnp.float32)
    after = from_behind(normed_cols[0:2], "tm", -1).astype(jnp.float32)
    padded = jnp.concatenate([before, wide, after], axis=0)
    convolved = jnp.zeros((frames_here, dancers_here, features_here), jnp.float32)
    for offset in range(KERNEL):
        convolved = convolved + conv_weight[offset] * padded[offset : offset + frames_here]
    return convolved


def begin(sems, pairs):
    copies = [
        pltpu.make_async_copy(source, target, sems.at[n]) for n, (source, target) in enumerate(pairs)
    ]
    for copy in copies:
        copy.start()
    return copies


def end(copies):
    for copy in copies:
        copy.wait()


def slot(index, size):
    return pl.ds(pl.multiple_of(index * size, size), size)


def dot(left, right):
    return jnp.dot(left, right, preferred_element_type=jnp.float32)


def normalise_kernel(n_ctx, mask_in, tokens, gain, full, own, mine, edge, mask, sems):
    rows, width = tokens.shape
    copies = begin(sems, [(mask_in, mask)])
    values = tokens[...].astype(jnp.float32)
    square = jnp.mean(values * values, axis=-1, keepdims=True)
    full[0:rows, :] = (values * lax.rsqrt(square + 1e-05) * gain[...]).astype(jnp.bfloat16)
    end(copies)
    entries = [
        jnp.full((8, LANES), mask[0, e].astype(jnp.float32), jnp.float32) for e in range(n_ctx)
    ]
    entries.append(jnp.zeros((8, width - n_ctx * LANES), jnp.float32))
    entries = jnp.concatenate(entries, axis=1).astype(jnp.bfloat16)
    full[rows:, :] = entries
    tm, tp = lax.axis_index("tm"), lax.axis_index("tp")
    own[...] = full[...]
    size, columns = edge.shape
    mine[...] = full[0:rows, slot(tp, columns)]
    edge[...] = jnp.where(tm == 0, mine[rows - size :, :], mine[0:size, :])


def pack_kernel(n_ctx, w_up, w_query, w_key, w_value, packed, sems):
    ctx, groups = lax.axis_index("ctx"), lax.axis_index("groups")
    count = packed.shape[0]
    pairs, column = [], 0
    for w in (w_up, w_query, w_key, w_value):
        size = w.shape[1] // n_ctx
        source = w.at[slot(groups, count), slot(ctx, size)]
        pairs.append((source, packed.at[:, column : column + size]))
        column += size
    end(begin(sems, pairs))


def split_kernel(block, piece):
    size = piece.shape[0]
    upper = lax.axis_index("tp") == 1
    piece[...] = jnp.where(upper, block[block.shape[0] - size :, :], block[0:size, :])


def pack_near_kernel(n_ctx, after, w_up, w_query, w_key, w_value, near, sems):
    ctx = lax.axis_index("ctx")
    pairs, column = [], 0
    for w in (w_up, w_query, w_key, w_value):
        size = w.shape[1] // n_ctx
        pairs.append((w.at[:, slot(ctx, size)], near.at[:, column : column + size]))
        column += size
    end(begin(sems, pairs))


def convolve_kernel(per_frame, tokens, mine, received, taps, last0, last1, base, held):
    tm, tp = lax.axis_index("tm"), lax.axis_index("tp")
    rows, columns = base.shape
    edge = 16
    margin = 2 * per_frame
    near = received[received.shape[0] - edge :, :].astype(jnp.float32)
    zeros = jnp.zeros((edge, columns), jnp.float32)
    held[0:edge, :] = jnp.where(tm == 1, near, zeros)
    held[edge : edge + rows, :] = mine[...].astype(jnp.float32)
    held[edge + rows :, :] = jnp.where(tm == 0, near, zeros)
    total = tokens[:, slot(tp, columns)].astype(jnp.float32)
    for offset in range(KERNEL):
        start = edge - margin + offset * per_frame
        total += taps[offset : offset + 1, :] * held[start : start + rows, :]
    base[...] = total


def project_kernel(n_ctx, *refs):
    own, block, other_block, piece, other_piece = refs[:5]
    near, far, farther = refs[5:8]
    acts = refs[8 : 8 + n_ctx]
    queries, keys, values, bias, held = refs[8 + n_ctx :]
    ctx, tm, groups, tp = (lax.axis_index(name) for name in AXES)
    rows, depth = own.shape[0] - 8, near.shape[0]
    sources = (
        (own, slot(0, rows), rows),
        (block, slot(1 + tp, rows), rows),
        (other_block, slot(2 - tp, rows), rows),
        (piece, slot(6 + tp, rows // 2), rows // 2),
        (other_piece, slot(7 - tp, rows // 2), rows // 2),
    )
    half = depth // 2
    cuts = ((0, slot(tm, depth), depth), (depth, slot(2 * (1 - tm) + groups, half), half))
    cuts += ((depth + half, slot(2 * (1 - tm) + 1 - groups, half), half),)
    for source, target, size in sources:
        for to, lanes, wide in cuts:
            held[target, to : to + wide] = source[0:size, lanes]
    total = dot(held[:, 0:depth], near[...])
    total += dot(held[:, depth : depth + half], far[...])
    total += dot(held[:, depth + half :], farther[...])
    hidden, wide = acts[0].shape[1], queries.shape[1]
    activated = jax.nn.gelu(total[:, :hidden], approximate=True).astype(jnp.bfloat16)
    for d in range(n_ctx):
        acts[d][...] = activated[d * rows : (d + 1) * rows]
    projected = total[:, hidden:].astype(jnp.bfloat16)
    queries[...] = projected[:, 0:wide]
    keys[...] = projected[:, wide : 2 * wide]
    values[...] = projected[:, 2 * wide :].T
    for j in range(n_ctx):
        lanes = slot(ctx ^ j, LANES)
        one, other = block[rows:, lanes], other_block[rows:, lanes]
        last, other_last = piece[rows // 2 :, lanes], other_piece[rows // 2 :, lanes]
        entries = (
            own[rows:, lanes],
            jnp.where(tp == 0, one, other),
            jnp.where(tp == 0, other, one),
            jnp.where(tp == 0, other_last, last),
        )
        for i, entry in enumerate(entries):
            flag = entry.astype(jnp.float32)
            target = slice(j * LANES, (j + 1) * LANES)
            bias[8 * i : 8 * (i + 1), target] = jnp.where(flag > 0, 0.0, MASKED)


def attend_kernel(n_ctx, blocks, *refs):
    count = len(blocks)
    acts, (queries, keys, values, bias) = refs[:count], refs[count : count + 4]
    outs = refs[count + 4 :]
    rows, hidden = acts[0].shape
    wide = outs[0].shape[1] - hidden
    lane_head = lax.broadcasted_iota(jnp.int32, (1, wide), 1) // HEAD_DIM
    for n, i in enumerate(blocks):
        block = queries[i * rows : (i + 1) * rows, :]
        allowed = jnp.concatenate(
            [
                jnp.broadcast_to(
                    bias[8 * i : 8 * i + 1, j * LANES : (j + 1) * LANES], (rows, rows)
                )
                for j in range(n_ctx)
            ],
            axis=0,
        )
        results = []
        for head in range(wide // HEAD_DIM):
            one = jnp.where(lane_head == head, block, jnp.zeros_like(block))
            scores = lax.dot_general(
                keys[...], one, (((1,), (1,)), ((), ())), preferred_element_type=jnp.float32
            )
            scores = scores * 0.125 + allowed
            peak = jnp.max(scores, axis=0, keepdims=True)
            expo = jnp.exp(scores - peak)
            total = jnp.sum(expo, axis=0, keepdims=True)
            mixed = dot(
                values[head * HEAD_DIM : (head + 1) * HEAD_DIM, :], expo.astype(jnp.bfloat16)
            )
            results.append(mixed / total)
        outs[n][:, 0:hidden] = acts[n][...]
        outs[n][:, hidden:] = jnp.concatenate(results, axis=0).T.astype(jnp.bfloat16)


def join_kernel(n_ctx, *refs):
    near_down, near_out, base = refs[:3]
    far_down, farther_down, far_out = refs[3:6]
    parts = refs[6 : 6 + n_ctx]
    keep, send, down, acts, atts = refs[6 + n_ctx :]
    ctx, tm, groups, tp = (lax.axis_index(name) for name in AXES)
    hidden, wide = acts.shape[1] // n_ctx, atts.shape[1] // n_ctx
    count, depth = farther_down.shape[0] - 16, near_out.shape[0]
    down[slot(groups, count), :] = far_down[0:count, :]
    down[slot(1 - groups, count), :] = farther_down[0:count, :]
    down[2 * count :, :] = far_out[depth:, :]
    for d in range(n_ctx):
        acts[:, slot(ctx ^ d, hidden)] = parts[d][:, 0:hidden]
        atts[:, slot(ctx ^ d, wide)] = parts[d][:, hidden:]
    near_sum = dot(acts[...], near_down[...]) + dot(atts[...], near_out[...])
    far_sum = dot(acts[...], down[...]) + dot(atts[...], far_out[0:depth, :])
    same = tm == tp
    keep[...] = jnp.where(same, near_sum, far_sum) + base[...]
    send[...] = jnp.where(same, far_sum, near_sum).astype(jnp.bfloat16)


def finish_kernel(keep, other, out):
    total = keep[...] + other[...].astype(jnp.float32)
    out[...] = total.reshape(out.shape).astype(jnp.bfloat16)


SMEM = pl.BlockSpec(memory_space=pltpu.SMEM)
VMEM = pl.BlockSpec(memory_space=pltpu.VMEM)
ANY = pl.BlockSpec(memory_space=pl.ANY)


def call(
    kernel, name, outs, ins, scratch=(), flops=0, moved=1 << 20, transcendentals=0, limit=8 << 20
):
    specs, values = zip(*ins)
    return pl.pallas_call(
        kernel,
        out_shape=[jax.ShapeDtypeStruct(shape, dtype) for shape, dtype in outs],
        in_specs=list(specs),
        out_specs=[VMEM] * len(outs),
        scratch_shapes=list(scratch),
        compiler_params=pltpu.CompilerParams(vmem_limit_bytes=limit),
        name=name,
        cost_estimate=pl.CostEstimate(
            flops=flops, bytes_accessed=moved, transcendentals=transcendentals
        ),
    )(*values)


def after(value, *others):
    return lax.optimization_barrier((value, others))[0]


def split_over_ctx(
    tokens, norm_gain, block_mask, w_query, w_key, w_value, w_out, w_up, w_down, conv_weight
):
    n_ctx = lax.axis_size("ctx")
    groups, ctx = lax.axis_index("groups"), lax.axis_index("ctx")
    tm, tp = lax.axis_index("tm"), lax.axis_index("tp")
    frames_here, dancers_here, width = tokens.shape
    rows = frames_here * dancers_here
    depth = w_query.shape[0]
    wide = w_query.shape[1] // n_ctx
    hidden = w_up.shape[1] // n_ctx
    columns = w_out.shape[1]
    packed = hidden + 3 * wide
    bf16, f32 = jnp.bfloat16, jnp.float32
    (packed_a,) = call(
        functools.partial(pack_kernel, n_ctx),
        "pack",
        [((depth // 2, packed), bf16)],
        [(ANY, w) for w in (w_up, w_query, w_key, w_value)],
        [pltpu.SemaphoreType.DMA((4,))],
        limit=(54 << 20) - (700 << 10),
    )
    token_rows = after(tokens, packed_a).reshape(rows, width)
    full, own, mine, edge = call(
        functools.partial(normalise_kernel, n_ctx),
        "normalise",
        [((rows + 8, width), bf16)] * 2 + [((rows, columns), bf16), ((16, columns), bf16)],
        [
            (ANY, block_mask[0]),
            (VMEM, token_rows),
            (VMEM, norm_gain.reshape(1, width)),
        ],
        [pltpu.SMEM((1, n_ctx), jnp.int32), pltpu.SemaphoreType.DMA((1,))],
    )
    x_a = across(packed_a, "tm", 1)
    y_a = across(x_a, "groups", 1)
    shared = w_down.shape[0] * 7 // 16
    sent_down = lax.dynamic_slice_in_dim(w_down, groups * shared, shared, 0)
    sent_down = jnp.concatenate([sent_down, edge], axis=0)
    x_down = across(after(sent_down, packed_a), "tm", 1)

    (near,) = call(
        functools.partial(pack_near_kernel, n_ctx),
        "pack_near",
        [((depth, packed), bf16)],
        [(ANY, w) for w in (packed_a, w_up, w_query, w_key, w_value)],
        [pltpu.SemaphoreType.DMA((4,))],
    )
    block = two_ways(full, (1, 2))
    other_block = across(block, "tp", 1)
    (piece,) = call(split_kernel, "split", [((rows // 2 + 8, width), bf16)], [(VMEM, block)])
    piece = two_ways(piece, (2, 1))
    other_piece = across(piece, "tp", 1)
    sent_out = jnp.concatenate([w_out, w_down[2 * shared :]], axis=0)
    x_out = across(after(sent_out, block), "tm", 1)
    *acts, queries, keys, values, bias = call(
        functools.partial(project_kernel, n_ctx),
        "project",
        [((rows, hidden), bf16)] * n_ctx
        + [((n_ctx * rows, wide), bf16)] * 2
        + [((wide, n_ctx * rows), bf16), ((8 * n_ctx, n_ctx * LANES), f32)],
        [(VMEM, value) for value in (own, block, other_block, piece, other_piece)]
        + [(VMEM, value) for value in (near, x_a, y_a)],
        [
            pltpu.VMEM((n_ctx * rows, width), bf16),
        ],
        flops=2 * n_ctx * rows * width * packed,
        moved=4 << 20,
        transcendentals=n_ctx * rows * hidden,
    )
    parts = [None] * n_ctx
    for blocks in ((2, 3, 1), (0,)):
        done = call(
            functools.partial(attend_kernel, n_ctx, blocks),
            "attend",
            [((rows, hidden + wide), bf16)] * len(blocks),
            [(VMEM, acts[i]) for i in blocks]
            + [(VMEM, value) for value in (queries, keys, values, bias)],
            flops=4 * len(blocks) * wide * n_ctx * rows * rows,
            transcendentals=len(blocks) * (wide // HEAD_DIM) * n_ctx * rows * rows,
        )
        for i, part in zip(blocks, done):
            parts[i] = part
    y_down = across(after(x_down, near), "groups", 1)
    parts = parts[:1] + [across(parts[i], "ctx", i) for i in range(1, n_ctx)]
    (base,) = call(
        functools.partial(convolve_kernel, dancers_here),
        "convolve",
        [((rows, columns), f32)],
        [
            (VMEM, token_rows),
            (VMEM, mine),
            (VMEM, x_down),
            (VMEM, conv_weight),
            (ANY, x_out),
            (ANY, parts[0]),
        ],
        [pltpu.VMEM((rows + 32, columns), f32)],
        flops=3000000000,
    )
    keep, send = call(
        functools.partial(join_kernel, n_ctx),
        "join",
        [((rows, columns), f32), ((rows, columns), bf16)],
        [(VMEM, w_down), (VMEM, w_out), (VMEM, base)]
        + [(VMEM, value) for value in (x_down, y_down, x_out)]
        + [(VMEM, value) for value in parts],
        [
            pltpu.VMEM(w_down.shape, bf16),
            pltpu.VMEM((rows, w_down.shape[0]), bf16),
            pltpu.VMEM((rows, w_out.shape[0]), bf16),
        ],
        flops=4 * rows * columns * n_ctx * (hidden + wide),
        moved=4 << 20,
    )
    other = across(send, "tp", 1)
    (denoised,) = call(
        finish_kernel,
        "finish",
        [((frames_here, dancers_here, columns), bf16)],
        [(VMEM, keep), (VMEM, other)],
    )
    return denoised


def gather_all(
    tokens, norm_gain, block_mask, w_query, w_key, w_value, w_out, w_up, w_down, conv_weight
):
    frames_here, dancers_here, width = tokens.shape
    rows_here = frames_here * dancers_here
    normed_grid = rms_norm(tokens, norm_gain)
    normed = normed_grid.reshape(rows_here, width)
    query_sum, key_sum, value_sum, hidden = tuple(
        jnp.dot(
            normed,
            lax.all_gather(piece, "tm", axis=0, tiled=True),
            preferred_element_type=jnp.float32,
        )
        for piece in (w_query, w_key, w_value, w_up)
    )
    local_heads = query_sum.shape[1] // HEAD_DIM
    queries = query_sum.astype(jnp.bfloat16).reshape(rows_here, local_heads, HEAD_DIM)
    grid = (frames_here, dancers_here, local_heads * HEAD_DIM)
    key_piece = lax.all_gather(
        key_sum.astype(jnp.bfloat16).reshape(grid), "ctx", axis=1, tiled=True
    )
    value_piece = lax.all_gather(
        value_sum.astype(jnp.bfloat16).reshape(grid), "ctx", axis=1, tiled=True
    )
    count = key_piece.shape[1]
    allowed = jnp.tile(jnp.repeat(block_mask[0, 0].astype(jnp.float32), dancers_here), frames_here)
    key_rows = key_piece.reshape(frames_here * count, local_heads, HEAD_DIM)
    value_rows = value_piece.reshape(frames_here * count, local_heads, HEAD_DIM)
    scores = (
        jnp.einsum("qhd,khd->hqk", queries, key_rows, preferred_element_type=jnp.float32) * 0.125
    )
    scores = jnp.where(allowed[None, None, :] > 0, scores, MASKED)
    expo = jnp.exp(scores - jnp.max(scores, axis=-1, keepdims=True)) * allowed[None, None, :]
    total = jnp.sum(expo, axis=-1)
    mixed = jnp.einsum(
        "hqk,khd->hqd", expo.astype(jnp.bfloat16), value_rows, preferred_element_type=jnp.float32
    )
    attended = (
        (mixed / total[:, :, None])
        .transpose(1, 0, 2)
        .reshape(rows_here, local_heads * HEAD_DIM)
        .astype(jnp.bfloat16)
    )
    activated = jax.nn.gelu(hidden, approximate=True).astype(jnp.bfloat16)
    out_full = lax.all_gather(w_out, "tm", axis=1, tiled=True)
    down_full = lax.all_gather(w_down, "tm", axis=1, tiled=True)
    branches = jnp.dot(attended, out_full, preferred_element_type=jnp.float32)
    branches = branches + jnp.dot(activated, down_full, preferred_element_type=jnp.float32)
    mine = lax.psum_scatter(
        branches.astype(jnp.bfloat16), "tp", scatter_dimension=1, tiled=True
    ).astype(jnp.float32)
    features_here = mine.shape[1]
    first_feature = lax.axis_index("tp") * features_here
    normed_cols = lax.dynamic_slice_in_dim(normed_grid, first_feature, features_here, 2)
    token_cols = lax.dynamic_slice_in_dim(tokens, first_feature, features_here, 2)
    result = (
        token_cols.astype(jnp.float32)
        + mine.reshape(frames_here, dancers_here, features_here)
        + convolve(normed_cols, conv_weight)
    )
    return result.astype(jnp.bfloat16)


def solution(mesh):
    n_ctx, n_tm = mesh.shape["ctx"], mesh.shape["tm"]

    def on_device(*arrays):
        local_heads = arrays[3].shape[1] // HEAD_DIM
        pairs = n_tm == 2 and mesh.shape["groups"] == 2 and mesh.shape["tp"] == 2
        even = n_ctx == 4 and local_heads == 2 * n_ctx
        chosen = split_over_ctx if pairs and even else gather_all
        return chosen(*arrays)

    placed = (
        P(("groups", "tm"), "ctx", None),
        P(),
        P(("groups", "tm"), "ctx", None),
        P("tm", "tp"),
        P("tm", "tp"),
        P("tm", "tp"),
        P("tp", "tm"),
        P("tm", "tp"),
        P("tp", "tm"),
        P(None, "tp"),
    )
    return jax.shard_map(
        on_device,
        mesh=mesh,
        in_specs=placed,
        out_specs=P(("groups", "tm"), "ctx", "tp"),
        check_vma=False,
    )
```
